32 devices in a mesh: seq: 8 (over y, x, core), batch: 4 (over z).
Axes of the slice: x: 2, y: 2, z: 4, core: 2. Of those that a mesh axis runs over, the one named last changes fastest.
Arguments:
- inputs: bfloat16 [16, 2048, 576], P('batch', 'seq'), may hold values from -6 to 6
- doc_lengths: int32 [16, 8], P('batch'), may hold values from 0 to 2048, as said below
- gain_one: bfloat16 [576], replicated, may hold values from 0.5 to 1.5
- gain_two: bfloat16 [576], replicated, may hold values from 0.5 to 1.5
- w_query: bfloat16 [576, 576], replicated, may hold values from -0.25 to 0.25
- w_key: bfloat16 [576, 192], replicated, may hold values from -0.25 to 0.25
- w_value: bfloat16 [576, 192], replicated, may hold values from -0.25 to 0.25
- w_out: bfloat16 [576, 576], replicated, may hold values from -1.75 to 1.75
- w_gate: bfloat16 [576, 1536], replicated, may hold values from -0.25 to 0.25
- w_up: bfloat16 [576, 1536], replicated, may hold values from -0.25 to 0.25
- w_down: bfloat16 [1536, 576], replicated, may hold values from -0.15625 to 0.15625
- cotangent: bfloat16 [16, 2048, 576], P('batch', 'seq'), may hold values from -6 to 6
Outputs:
- output: bfloat16 [16, 2048, 576], P('batch', 'seq')
- input_grad: float32 [16, 2048, 576], P('batch', 'seq')
- gain_one_grad: float32 [576], replicated
- gain_two_grad: float32 [576], replicated
- w_query_grad: float32 [576, 576], replicated
- w_key_grad: float32 [576, 192], replicated
- w_value_grad: float32 [576, 192], replicated
- w_out_grad: float32 [576, 576], replicated
- w_gate_grad: float32 [576, 1536], replicated
- w_up_grad: float32 [576, 1536], replicated
- w_down_grad: float32 [1536, 576], replicated
The draws below stay inside these ranges and needn't reach their ends.
Inputs may be any that keep to these rules, and one draw needn't show every extreme that they name: `doc_lengths`: in every row the entries are multiples of 128 and add up to 2048; the nonzero ones come first; some row is a single document of 2048 positions.
All inputs are finite; a program needn't handle non-finite values.
Results may differ from the reference program's by a relative error of at most 0.018.
Values may be sent and summed in bfloat16 or wider, within the bound.
No kernel may reach another device: no remote copies, remote signals or barrier semaphores. Data moves between devices by JAX's collectives and lax.ppermute only.
A program may use at most 192 MiB of HBM per device.

```python
import math
import jax
import jax.numpy as jnp
from jax import lax

D = 576
HEADS = 9
KV_HEADS = 3
HEAD = 64
FF = 1536
DOCS = 8
LENGTH = 2048
ROWS = 16


def draw_doc_lengths(key, part):
    grain = LENGTH // 16
    key_count, key_single, key_cuts = jax.random.split(key, 3)
    counts = jax.random.randint(key_count, (ROWS,), 1, DOCS + 1)
    single = jax.random.randint(key_single, (), 0, ROWS)
    counts = jnp.where(jnp.arange(ROWS) == single, 1, counts)
    row_keys = jax.random.split(key_cuts, ROWS)
    cuts = jax.vmap(lambda row_key: jax.random.permutation(row_key, 15)[:DOCS - 1] + 1)(row_keys)
    used = jnp.arange(DOCS - 1)[None, :] < counts[:, None] - 1
    cuts = jnp.sort(jnp.where(used, cuts, 16), axis=1)
    bounds = jnp.concatenate([jnp.zeros((ROWS, 1), jnp.int32), cuts.astype(jnp.int32), jnp.full((ROWS, 1), 16, jnp.int32)], axis=1)
    return ((bounds[:, 1:] - bounds[:, :-1]) * grain).astype(jnp.int32)


def block_levels(stream_key, shape, cuts, least, high):
    def one(position, parts):
        draws = jax.random.uniform(jax.random.fold_in(jax.random.fold_in(stream_key, 6), position), (parts,), jnp.float32, least / len(cuts), high / len(cuts))
        return jnp.repeat(jnp.exp(draws), shape[position] // parts).reshape((-1,) + (1,) * (len(shape) - position - 1))

    level = one(*cuts[0])
    for cut in cuts[1:]:
        level = level * one(*cut)
    return level


def scatter_about(stream_key, shape, spread, bound, shards=(), kind=jnp.bfloat16):
    entries = spread * jax.random.normal(stream_key, shape, jnp.float32)
    if shards:
        entries = entries * block_levels(stream_key, shape, shards, -0.22, 0.18)
    return jnp.clip(entries, -bound, bound).astype(kind)


def setup_inputs(seed: int = 0) -> dict:
    key_of = jax.random.split(jax.random.key(seed), 13)
    inputs = scatter_about(key_of[0], (ROWS, LENGTH, D), 1.0, 6.0, ((0, 4), (1, 8)))
    doc_lengths = draw_doc_lengths(jax.random.fold_in(key_of[12], 71), 0)
    gain_one = jnp.clip(1.0 + 0.1 * jax.random.normal(key_of[2], (D,), jnp.float32), 0.5, 1.5).astype(jnp.bfloat16)
    gain_two = jnp.clip(1.0 + 0.1 * jax.random.normal(key_of[3], (D,), jnp.float32), 0.5, 1.5).astype(jnp.bfloat16)
    w_query = scatter_about(key_of[4], (D, D), D ** -0.5, 0.25)
    w_key = scatter_about(key_of[5], (D, KV_HEADS * HEAD), D ** -0.5, 0.25)
    w_value = scatter_about(key_of[6], (D, KV_HEADS * HEAD), D ** -0.5, 0.25)
    w_out = scatter_about(key_of[7], (D, D), (D // 48) ** -0.5, 1.75)
    w_gate = scatter_about(key_of[8], (D, FF), D ** -0.5, 0.25)
    w_up = scatter_about(key_of[9], (D, FF), D ** -0.5, 0.25)
    w_down = scatter_about(key_of[10], (FF, D), FF ** -0.5, 0.15625)
    cotangent = scatter_about(key_of[11], (ROWS, LENGTH, D), 1.0, 6.0, ((0, 4), (1, 8)))
    return dict(inputs=inputs, doc_lengths=doc_lengths, gain_one=gain_one, gain_two=gain_two, w_query=w_query, w_key=w_key, w_value=w_value, w_out=w_out, w_gate=w_gate, w_up=w_up, w_down=w_down, cotangent=cotangent)


@jax.custom_vjp
def low(v):
    return lax.optimization_barrier(v.astype(jnp.bfloat16)).astype(jnp.float32)

@jax.custom_vjp
def low_back(v):
    return v

def low_keep(v):
    return (low(v), None)

def low_pass(kept, grad):
    return (grad,)

def back_keep(v):
    return (v, None)

def back_low(kept, grad):
    return (low(grad),)
low.defvjp(low_keep, low_pass)
low_back.defvjp(back_keep, back_low)
EPSILON = 1e-05
ROPE_BASE = 10000.0
FAR_NEGATIVE = -1e+30

def hdot(left_side, right_side):
    return jnp.dot(left_side, right_side, precision=lax.Precision.HIGHEST, preferred_element_type=jnp.float32)

def rms_factor(values):
    return lax.rsqrt(lax.optimization_barrier(jnp.mean(values * values, axis=-1, keepdims=True)) + EPSILON)

def doc_layout(row_lengths, places):
    doc_ends = jnp.cumsum(row_lengths)
    before = doc_ends[None, :] <= places[:, None]
    documents = lax.optimization_barrier(jnp.sum(before.astype(jnp.int32), axis=1))
    starts = lax.optimization_barrier(jnp.sum(jnp.where(before, row_lengths[None, :], 0), axis=1))
    return (documents, places - starts)

def rotate(values, positions, heads_count):
    halfway = HEAD // 2
    inverse = 1.0 / ROPE_BASE ** (jnp.arange(halfway, dtype=jnp.float32) * (2.0 / HEAD))
    angles = positions.astype(jnp.float32)[:, None] * inverse[None, :]
    cosine_table = jnp.cos(angles)[:, None, :]
    sine_table = jnp.sin(angles)[:, None, :]
    shaped = values.reshape(values.shape[0], heads_count, HEAD)
    first_half = shaped[..., :halfway]
    second_half = shaped[..., halfway:]
    result = jnp.concatenate([first_half * cosine_table - second_half * sine_table, second_half * cosine_table + first_half * sine_table], axis=-1)
    return result.reshape(values.shape)

def layer_row(row_input, row_lengths, gain_one, gain_two, w_query, w_key, w_value, w_out, w_gate, w_up, w_down):
    places = jnp.arange(LENGTH, dtype=jnp.int32)
    documents, positions = doc_layout(row_lengths, places)
    groups = HEADS // KV_HEADS
    score_scale = 1.0 / math.sqrt(HEAD)
    normed_one = low(row_input * rms_factor(row_input) * gain_one)
    queries = low(rotate(low_back(hdot(normed_one, w_query)), positions, HEADS))
    keys_rot = low(rotate(low_back(hdot(normed_one, w_key)), positions, KV_HEADS))
    values_low = low(low_back(hdot(normed_one, w_value)))
    query_heads = queries.reshape(LENGTH, KV_HEADS, groups, HEAD)
    key_heads = keys_rot.reshape(LENGTH, KV_HEADS, HEAD)
    value_heads = values_low.reshape(LENGTH, KV_HEADS, HEAD)
    scores = low_back(jnp.einsum('qhgd,khd->hgqk', query_heads, key_heads, precision=lax.Precision.HIGHEST) * score_scale)
    allowed = (documents[:, None] == documents[None, :]) & (places[None, :] <= places[:, None])
    scores = jnp.where(allowed[None, None], scores, FAR_NEGATIVE)
    row_top = lax.optimization_barrier(jnp.max(scores, axis=-1, keepdims=True))
    expd = jnp.exp(scores - row_top)
    weights_soft = low(expd / lax.optimization_barrier(jnp.sum(expd, axis=-1, keepdims=True)))
    mixed = jnp.einsum('hgqk,khd->qhgd', weights_soft, value_heads, precision=lax.Precision.HIGHEST).reshape(LENGTH, D)
    mixed = low(low_back(mixed))
    branch = low_back(hdot(mixed, w_out))
    middle = row_input + branch
    normed_two = low(middle * rms_factor(middle) * gain_two)
    gate_proj = low_back(hdot(normed_two, w_gate))
    up_proj = low_back(hdot(normed_two, w_up))
    hidden = low(gate_proj * jax.nn.sigmoid(gate_proj) * up_proj)
    return middle + low_back(hdot(hidden, w_down))

def reference(inputs, doc_lengths, gain_one, gain_two, w_query, w_key, w_value, w_out, w_gate, w_up, w_down, cotangent):
    floats = [value.astype(jnp.float32) for value in (inputs, gain_one, gain_two, w_query, w_key, w_value, w_out, w_gate, w_up, w_down)]

    def forward(row_stack, gain_a, gain_b, query_w, key_w, value_w, out_w, gate_w, up_w, down_w):

        def per_row(row_pair):
            return jax.checkpoint(layer_row)(row_pair[0], row_pair[1], gain_a, gain_b, query_w, key_w, value_w, out_w, gate_w, up_w, down_w)
        return lax.map(per_row, (row_stack, doc_lengths))
    output, pull_back = jax.vjp(forward, *floats)
    grads = pull_back(cotangent.astype(jnp.float32))
    return (output.astype(jnp.bfloat16), grads[0], grads[1], grads[2], grads[3], grads[4], grads[5], grads[6], grads[7], grads[8], grads[9])
```

```python
import functools
import math

import jax
import jax.numpy as jnp
from jax import lax
from jax.experimental import pallas as pl
from jax.experimental.pallas import tpu as pltpu
from jax.sharding import PartitionSpec as P

HEADS = 9
KV_HEADS = 3
HEAD = 64
GROUPS = HEADS // KV_HEADS
HALF = HEAD // 2
EPSILON = 1e-05
ROPE_BASE = 10000.0
FAR_NEGATIVE = -1e30
SUM_ROWS = 16

F32 = jnp.float32
BF16 = jnp.bfloat16
VMEM_LIMIT = 56 * 1024 * 1024


def rms_factor(values):
    return lax.rsqrt(jnp.mean(values * values, axis=-1, keepdims=True) + EPSILON)


def norm_back(source, factor, gain_value, upstream):
    scaled = upstream * gain_value
    return factor * scaled - source * factor * factor * factor * jnp.mean(
        scaled * source, axis=-1, keepdims=True
    )


def mdot(left, right):
    return jnp.dot(left, right, preferred_element_type=F32)


def tdot(left, right):
    return lax.dot_general(left, right, (((0,), (0,)), ((), ())), preferred_element_type=F32)


def rdot(left, right):
    return lax.dot_general(left, right, (((1,), (1,)), ((), ())), preferred_element_type=F32)


def call(body, outs, scratch=(), smem=0, count=0, cost=None, **more):
    in_specs = [pl.BlockSpec(memory_space=pltpu.SMEM)] * smem
    in_specs += [pl.BlockSpec(memory_space=pltpu.VMEM)] * (count - smem)
    return pl.pallas_call(
        body,
        out_shape=[jax.ShapeDtypeStruct(*o) for o in outs],
        in_specs=in_specs,
        out_specs=[pl.BlockSpec(memory_space=pltpu.VMEM)] * len(outs),
        scratch_shapes=list(scratch),
        compiler_params=pltpu.CompilerParams(vmem_limit_bytes=VMEM_LIMIT),
        cost_estimate=cost,
        **more,
    )


def estimate(flops, nbytes, trans=0):
    return pl.CostEstimate(
        flops=int(flops), bytes_accessed=int(nbytes), transcendentals=int(trans)
    )


def project_body(x_ref, gain_ref, w_ref, cos_ref, sin_ref, q_ref, kv_ref):
    tokens = x_ref.shape[0]
    x = x_ref[...].astype(F32)
    normed = (x * rms_factor(x) * gain_ref[...]).astype(BF16)
    turned = rdot(w_ref[...], normed)
    cos, sin = cos_ref[...], sin_ref[...]
    for head in range(HEADS):
        a = turned[head * HEAD : head * HEAD + HALF]
        b = turned[head * HEAD + HALF : (head + 1) * HEAD]
        kv, lane = head // GROUPS, (head % GROUPS) * tokens
        q_ref[kv, :HALF, lane : lane + tokens] = ((a * cos - b * sin) * 0.125).astype(BF16)
        q_ref[kv, HALF:, lane : lane + tokens] = ((b * cos + a * sin) * 0.125).astype(BF16)
    base = HEADS * HEAD
    for head in range(KV_HEADS):
        at = base + head * HEAD
        a, b = turned[at : at + HALF], turned[at + HALF : at + HEAD]
        kv_ref[head, :HALF, :] = (a * cos - b * sin).astype(BF16)
        kv_ref[head, HALF:HEAD, :] = (b * cos + a * sin).astype(BF16)
        at += KV_HEADS * HEAD
        kv_ref[head, HEAD:, :] = turned[at : at + HEAD].astype(BF16)


def owner(block, parts):
    group, place = block // parts, block % parts
    return jnp.where(group % 2 == 0, place, parts - 1 - place)


def slot_of(block, info, parts, rows):
    relative = (owner(block, parts) - info[1] + parts) % parts
    return relative * rows + ((block // parts) ^ info[0])


def visible(block, start, place, shape):
    key_place = block * shape[0] + lax.broadcasted_iota(jnp.int32, shape, 0)
    return (key_place >= start) & (key_place <= place)


def attend_body(parts, rows, info_ref, start_ref, place_ref, *refs):
    q_refs, refs = refs[:rows], refs[rows:]
    kv_refs, refs = refs[: rows * parts], refs[rows * parts :]
    o_ref, lse_ref, k_nat, v_aug, acc = refs
    tokens = kv_refs[0].shape[-1]
    info = (info_ref[0], info_ref[1])
    ones = (lax.broadcasted_iota(jnp.int32, (SUM_ROWS, tokens), 0) == 0).astype(BF16)
    for slot, kv_ref in enumerate(kv_refs):
        for head in range(KV_HEADS):
            k_nat[slot, head] = kv_ref[head, :HEAD, :].T
            v_aug[slot, head, :HEAD, :] = kv_ref[head, HEAD:, :]
            v_aug[slot, head, HEAD:, :] = ones

    for row in range(rows):
        mine, low, full = info_ref[2 + 3 * row], info_ref[3 + 3 * row], info_ref[4 + 3 * row]
        acc[...] = jnp.zeros_like(acc)
        start, place = start_ref[row], place_ref[row]

        def step(block, tops, masked):
            slot = slot_of(block, info, parts, rows)
            allowed = visible(block, start, place, (tokens, start.shape[-1])) if masked else None
            result = []
            for head in range(KV_HEADS):
                scores = mdot(k_nat[slot, head], q_refs[row][head])
                if masked:
                    scores = jnp.where(allowed, scores, FAR_NEGATIVE)
                top = jnp.maximum(tops[head], jnp.max(scores, axis=0, keepdims=True))
                weights = jnp.exp(scores - top).astype(BF16)
                acc[head] = acc[head] * jnp.exp(tops[head] - top) + mdot(v_aug[slot, head], weights)
                result.append(top)
            return tuple(result)

        tops = tuple(
            jnp.full((1, start.shape[-1]), FAR_NEGATIVE, F32) for unused in range(KV_HEADS)
        )
        middle = jnp.minimum(full, mine)
        tops = lax.fori_loop(low, middle, lambda b, s: step(b, s, True), tops)
        tops = lax.fori_loop(middle, mine, lambda b, s: step(b, s, False), tops)
        tops = step(mine, tops, True)
        for head in range(KV_HEADS):
            mass = acc[head, HEAD : HEAD + 1, :]
            o_ref[row, head] = (acc[head, :HEAD, :] / mass).astype(BF16)
            lse_ref[row, head] = tops[head] + jnp.log(mass)


def attend_back_body(parts, rows, info_ref, start_ref, place_ref, cos_ref, sin_ref, lse_ref, delta_ref, do_ref, *refs):
    q_refs, refs = refs[:rows], refs[rows:]
    kv_refs, refs = refs[: rows * parts], refs[rows * parts :]
    dq_ref, own_ref = refs[:2]
    other_refs = refs[2 : 1 + parts]
    k_nat, v_nat, k_turned, pair, dq_acc, dkv = refs[1 + parts :]
    tokens = kv_refs[0].shape[-1]
    wide = GROUPS * tokens
    info = (info_ref[0], info_ref[1])
    for slot, kv_ref in enumerate(kv_refs):
        for head in range(KV_HEADS):
            k_nat[slot, head] = kv_ref[head, :HEAD, :].T
            v_nat[slot, head] = kv_ref[head, HEAD:, :].T
            k_turned[slot, head] = kv_ref[head, :HEAD, :]
    dkv[...] = jnp.zeros_like(dkv)
    blank = jnp.zeros((wide, HEAD), BF16)

    for row in range(rows):
        mine, low, full = info_ref[2 + 3 * row], info_ref[3 + 3 * row], info_ref[4 + 3 * row]
        dq_acc[...] = jnp.zeros_like(dq_acc)
        start, place = start_ref[row], place_ref[row]
        for head in range(KV_HEADS):
            pair[head, :wide, :] = jnp.concatenate([q_refs[row][head].T, blank], axis=1)
            pair[head, wide:, :] = jnp.concatenate([blank, do_ref[row, head].T], axis=1)

        def step(block, masked):
            slot = slot_of(block, info, parts, rows)
            allowed = visible(block, start, place, (tokens, wide)) if masked else None
            for head in range(KV_HEADS):
                scores = mdot(k_nat[slot, head], q_refs[row][head])
                weights = jnp.exp(scores - lse_ref[row, head])
                if masked:
                    weights = jnp.where(allowed, weights, 0.0)
                back = mdot(v_nat[slot, head], do_ref[row, head])
                slope = (weights * (back - delta_ref[row, head])).astype(BF16)
                dq_acc[head] += mdot(k_turned[slot, head], slope)
                both = jnp.concatenate([slope, weights.astype(BF16)], axis=1)
                dkv[slot, head] += mdot(both, pair[head])

        def loop(first, last, masked):
            def once(block, carry):
                step(block, masked)
                return carry

            lax.fori_loop(first, last, once, 0)

        middle = jnp.minimum(full, mine)
        loop(low, middle, True)
        loop(middle, mine, False)
        step(mine, True)
        cos, sin = cos_ref[row], sin_ref[row]
        for head in range(KV_HEADS):
            for group in range(GROUPS):
                lanes = slice(group * tokens, (group + 1) * tokens)
                a = dq_acc[head, :HALF, lanes] * 0.125
                b = dq_acc[head, HALF:, lanes] * 0.125
                dq_ref[row, head, :HALF, lanes] = (a * cos + b * sin).astype(BF16)
                dq_ref[row, head, HALF:, lanes] = (b * cos - a * sin).astype(BF16)
    own_ref[...] = dkv[:rows]
    for i, other_ref in enumerate(other_refs):
        other_ref[...] = dkv[(i + 1) * rows : (i + 2) * rows].astype(BF16)


def stacked(ref, tokens):
    pieces = []
    for head in range(HEADS):
        lane = (head % GROUPS) * tokens
        pieces.append(ref[0, head // GROUPS, :, lane : lane + tokens])
    return jnp.concatenate(pieces, axis=0)


def feed_body(
    o_ref, x_ref, g_ref, gain_ref, wo_ref, wg_ref, wu_ref, wd_ref,
    out_ref, h_ref, hid_ref, dgate_ref, dup_ref, dmid_ref, do_ref, delta_ref, two_ref, wog_ref,
):
    tokens = x_ref.shape[1]
    first = pl.program_id(0) == 0
    attended = stacked(o_ref, tokens)
    middle = x_ref[0].astype(F32) + tdot(attended, wo_ref[...])
    factor = rms_factor(middle)
    gain = gain_ref[...]
    normed = (middle * factor * gain).astype(BF16)
    h_ref[0] = normed
    gate = mdot(normed, wg_ref[...])
    up = mdot(normed, wu_ref[...])
    sig = jax.nn.sigmoid(gate)
    silu = gate * sig
    hidden = (silu * up).astype(BF16)
    hid_ref[0] = hidden
    out_ref[0] = (middle + mdot(hidden, wd_ref[...])).astype(BF16)
    grad = g_ref[0]
    dhidden = rdot(grad, wd_ref[...])
    dgate = (dhidden * up * sig * (1.0 + gate * (1.0 - sig))).astype(BF16)
    dup = (dhidden * silu).astype(BF16)
    dgate_ref[0] = dgate
    dup_ref[0] = dup
    dnormed = rdot(dgate, wg_ref[...]) + rdot(dup, wu_ref[...])
    two = jnp.sum(dnormed * middle * factor, axis=0, keepdims=True)
    dmiddle = grad.astype(F32) + norm_back(middle, factor, gain, dnormed)
    dmid_ref[0] = dmiddle
    branch = dmiddle.astype(BF16)
    out_grad = mdot(attended, branch)

    @pl.when(first)
    def _():
        two_ref[...] = two
        wog_ref[...] = out_grad

    @pl.when(jnp.logical_not(first))
    def _():
        two_ref[...] += two
        wog_ref[...] += out_grad

    dattended = rdot(wo_ref[...], branch).astype(BF16)
    product = dattended.astype(F32) * attended.astype(F32)
    for head in range(HEADS):
        kv, lane = head // GROUPS, (head % GROUPS) * tokens
        rows = slice(head * HEAD, (head + 1) * HEAD)
        do_ref[0, kv, :, lane : lane + tokens] = dattended[rows]
        delta_ref[0, kv, :, lane : lane + tokens] = jnp.sum(product[rows], axis=0, keepdims=True)


def feed(o, x, g, gain, wo, wg, wu, wd):
    rows, tokens, width = x.shape
    hidden = wg.shape[1]
    wide = GROUPS * tokens

    def whole(*shape):
        return pl.BlockSpec(shape, lambda i: (0,) * len(shape))

    def part(*shape):
        return pl.BlockSpec((1, *shape), lambda i: (i,) + (0,) * len(shape))

    return pl.pallas_call(
        feed_body,
        grid=(rows,),
        in_specs=[
            part(KV_HEADS, HEAD, wide), part(tokens, width), part(tokens, width), whole(1, width),
            whole(width, width), whole(width, hidden), whole(width, hidden), whole(hidden, width),
        ],
        out_specs=[
            part(tokens, width), part(tokens, width), part(tokens, hidden), part(tokens, hidden),
            part(tokens, hidden), part(tokens, width), part(KV_HEADS, HEAD, wide),
            part(KV_HEADS, 1, wide), whole(1, width), whole(width, width),
        ],
        out_shape=[
            jax.ShapeDtypeStruct((rows, tokens, width), BF16),
            jax.ShapeDtypeStruct((rows, tokens, width), BF16),
            jax.ShapeDtypeStruct((rows, tokens, hidden), BF16),
            jax.ShapeDtypeStruct((rows, tokens, hidden), BF16),
            jax.ShapeDtypeStruct((rows, tokens, hidden), BF16),
            jax.ShapeDtypeStruct((rows, tokens, width), F32),
            jax.ShapeDtypeStruct((rows, KV_HEADS, HEAD, wide), BF16),
            jax.ShapeDtypeStruct((rows, KV_HEADS, 1, wide), F32),
            jax.ShapeDtypeStruct((1, width), F32),
            jax.ShapeDtypeStruct((width, width), F32),
        ],
        compiler_params=pltpu.CompilerParams(vmem_limit_bytes=VMEM_LIMIT),
        cost_estimate=estimate(2 * rows * tokens * 7.3e6, 4e7, rows * tokens * hidden),
    )(o, x, g, gain, wo, wg, wu, wd)


def last_body(
    parts, dq_ref, own_ref, x_ref, dmid_ref, gain_ref, wq_ref, wkv_ref, cos_ref, ahead_ref, behind_ref, *refs
):
    other_refs = refs[: parts - 1]
    ig_ref, dq_out, dkv_out, h_ref, one_ref = refs[parts - 1 :]
    tokens = x_ref.shape[1]
    first = pl.program_id(0) == 0
    x = x_ref[0].astype(F32)
    factor = rms_factor(x)
    gain = gain_ref[...]
    h_ref[0] = (x * factor * gain).astype(BF16)
    dq = stacked(dq_ref, tokens).T
    dq_out[0] = dq
    dnormed = mdot(dq, wq_ref[...])
    cos, ahead, behind = cos_ref[0], ahead_ref[0], behind_ref[0]
    pieces = []
    for head in range(KV_HEADS):
        total = own_ref[0, head]
        for other_ref in other_refs:
            total = total + other_ref[0, head].astype(F32)
        turned = (
            total * cos
            + pltpu.roll(total, 2 * HEAD - HALF, 1) * ahead
            + pltpu.roll(total, HALF, 1) * behind
        )
        pieces.append(turned.astype(BF16))
    dkv = jnp.concatenate(pieces, axis=1)
    dkv_out[0] = dkv
    dnormed = dnormed + mdot(dkv, wkv_ref[...])
    one = jnp.sum(dnormed * x * factor, axis=0, keepdims=True)

    @pl.when(first)
    def _():
        one_ref[...] = one

    @pl.when(jnp.logical_not(first))
    def _():
        one_ref[...] += one

    ig_ref[0] = (dmid_ref[0] + norm_back(x, factor, gain, dnormed)).astype(BF16)


def last(dq, own, others, x, dmid, gain, wq_t, wkv_t, cos, ahead, behind):
    rows, tokens, width = x.shape
    wide = GROUPS * tokens
    pair = 2 * HEAD
    parts = len(others) + 1

    def whole(*shape):
        return pl.BlockSpec(shape, lambda i: (0,) * len(shape))

    def part(*shape):
        return pl.BlockSpec((1, *shape), lambda i: (i,) + (0,) * len(shape))

    return pl.pallas_call(
        functools.partial(last_body, parts),
        grid=(rows,),
        in_specs=[
            part(KV_HEADS, HEAD, wide), part(KV_HEADS, tokens, pair), part(tokens, width),
            part(tokens, width), whole(1, width), whole(width, width), whole(KV_HEADS * pair, width),
            part(tokens, pair), part(tokens, pair), part(tokens, pair),
            *[part(KV_HEADS, tokens, pair) for unused in others],
        ],
        out_specs=[
            part(tokens, width), part(tokens, width), part(tokens, KV_HEADS * pair),
            part(tokens, width), whole(1, width),
        ],
        out_shape=[
            jax.ShapeDtypeStruct((rows, tokens, width), BF16),
            jax.ShapeDtypeStruct((rows, tokens, width), BF16),
            jax.ShapeDtypeStruct((rows, tokens, KV_HEADS * pair), BF16),
            jax.ShapeDtypeStruct((rows, tokens, width), BF16),
            jax.ShapeDtypeStruct((1, width), F32),
        ],
        compiler_params=pltpu.CompilerParams(vmem_limit_bytes=VMEM_LIMIT),
        cost_estimate=estimate(2 * rows * tokens * 5.6e5, 1.2e7),
    )(dq, own, x, dmid, gain, wq_t, wkv_t, cos, ahead, behind, *others)


def halve_axis(shape):
    if (shape[0] // 2) % 8 == 0 and shape[0] % 2 == 0:
        return 0
    if (shape[1] // 2) % 128 == 0 and shape[1] % 2 == 0:
        return 1
    return 0


def swap(value, axis, bit):
    size = lax.axis_size(axis)
    return lax.ppermute(value, axis, [(i, i ^ bit) for i in range(size)])


def scatter_sum(value, steps):
    cuts = []
    for axis, bit in steps:
        dim = halve_axis(value.shape)
        half = value.shape[dim] // 2
        mine = (lax.axis_index(axis) // bit) % 2
        keep = lax.dynamic_slice_in_dim(value, mine * half, half, dim)
        send = lax.dynamic_slice_in_dim(value, (1 - mine) * half, half, dim)
        got = swap(send, axis, bit)
        value = (keep.astype(F32) + got.astype(F32)).astype(BF16)
        cuts.append((axis, bit, dim, mine))
    return value, cuts


def gather_back(value, cuts):
    for axis, bit, dim, mine in reversed(cuts):
        got = swap(value, axis, bit)
        first = jnp.where(mine == 0, value, got)
        second = jnp.where(mine == 0, got, value)
        value = jnp.concatenate([first, second], axis=dim)
    return value


def shards(
    inputs, doc_lengths, gain_one, gain_two, w_query, w_key, w_value, w_out, w_gate, w_up, w_down, cotangent
):
    rows, tokens, width = inputs.shape
    seq = lax.axis_size("seq")
    batch = lax.axis_size("batch")
    parts = seq // rows
    me = lax.axis_index("seq")
    group, part = me // parts, me % parts
    wide = GROUPS * tokens
    kv_width = KV_HEADS * HEAD

    def dealt(block):
        g, place = block // parts, block % parts
        return g, place if g % 2 == 0 else parts - 1 - place

    def route(step):
        pairs = []
        for block in range(seq):
            g, p = dealt(block)
            pairs.append((block, (g ^ step) * parts + p))
        return pairs

    def bring(value):
        return [
            lax.ppermute(
                lax.dynamic_index_in_dim(value, group ^ step, 0, keepdims=False), "seq", route(step)
            )
            for step in range(rows)
        ]

    def back(value):
        return [
            lax.ppermute(value[step], "seq", [(b, a) for a, b in route(step)])
            for step in range(rows)
        ]

    def place_rows(pieces, dtype):
        whole = jnp.zeros((rows, tokens, width), dtype)
        for step, piece in enumerate(pieces):
            whole = lax.dynamic_update_index_in_dim(whole, piece.astype(dtype), group ^ step, 0)
        return whole

    x_parts = bring(inputs)
    held = lax.optimization_barrier((cotangent, *x_parts))
    x_parts = list(held[1:])
    g_parts = bring(held[0])

    groups_here = group ^ jnp.arange(rows, dtype=jnp.int32)
    blocks = groups_here * parts + jnp.where(groups_here % 2 == 0, part, parts - 1 - part)
    lengths = lax.dynamic_index_in_dim(doc_lengths, group, 0, keepdims=False)
    docs = lengths.shape[0]
    order = jnp.arange(docs)
    ends = jnp.sum(jnp.where(order[None, :] <= order[:, None], lengths[None, :], 0), axis=1)
    places = blocks[:, None] * tokens + jnp.arange(tokens, dtype=jnp.int32)[None, :]
    starts = jnp.sum(jnp.where(ends <= places[..., None], lengths, 0), axis=-1)
    info = jnp.concatenate(
        [
            jnp.stack([group, part]),
            jnp.stack(
                [blocks, starts[:, 0] // tokens, (starts[:, -1] + tokens - 1) // tokens], axis=1
            ).reshape(-1),
        ]
    ).astype(jnp.int32)
    inverse = 1.0 / ROPE_BASE ** (jnp.arange(HALF, dtype=F32) * (2.0 / HEAD))
    angles = (places - starts).astype(F32)[:, None, :] * inverse[None, :, None]
    cos_t, sin_t = jnp.cos(angles), jnp.sin(angles)
    cos_n, sin_n = jnp.swapaxes(cos_t, 1, 2), jnp.swapaxes(sin_t, 1, 2)
    still = jnp.zeros((rows, tokens, HEAD), F32)
    nought = jnp.zeros_like(sin_n)
    cos_n = jnp.concatenate([cos_n, cos_n, still + 1.0], axis=-1)
    ahead = jnp.concatenate([sin_n, nought, still], axis=-1)
    behind = jnp.concatenate([nought, -sin_n, still], axis=-1)
    start_w = jnp.tile(starts[:, None, :], (1, 1, GROUPS))
    place_w = jnp.tile(places[:, None, :], (1, 1, GROUPS))
    gain_a = gain_one.astype(F32)[None, :]
    gain_b = gain_two.astype(F32)[None, :]
    w_turned = jnp.concatenate([w_query, w_key, w_value], axis=1).T
    wq_t = w_query.T
    wkv_t = jnp.concatenate(
        [w_key.reshape(width, KV_HEADS, HEAD), w_value.reshape(width, KV_HEADS, HEAD)], axis=2
    ).reshape(width, 2 * kv_width).T

    project = call(
        project_body,
        [((KV_HEADS, HEAD, wide), BF16), ((KV_HEADS, 2 * HEAD, tokens), BF16)],
        count=5,
        cost=estimate(2 * tokens * width * (width + 2 * kv_width), 2e6),
    )
    q_parts, kv_parts = [], []
    for i in range(rows):
        q, kv = project(x_parts[i], gain_a, w_turned, cos_t[i], sin_t[i])
        q_parts.append(q)
        kv_parts.append(kv)

    def ring(i, value):
        pairs = [
            (r * parts + (p + i) % parts, r * parts + p) for r in range(rows) for p in range(parts)
        ]
        return lax.ppermute(value, "seq", pairs)

    kv_all = list(kv_parts)
    for i in range(1, parts):
        kv_all += [ring(i, kv) for kv in kv_parts]
    slots = rows * parts
    pair_work = rows * (seq + 1) / 2 * tokens * tokens * HEADS * HEAD
    o, lse = call(
        functools.partial(attend_body, parts, rows),
        [((rows, KV_HEADS, HEAD, wide), BF16), ((rows, KV_HEADS, 1, wide), F32)],
        scratch=[
            pltpu.VMEM((slots, KV_HEADS, tokens, HEAD), BF16),
            pltpu.VMEM((slots, KV_HEADS, HEAD + SUM_ROWS, tokens), BF16),
            pltpu.VMEM((KV_HEADS, HEAD + SUM_ROWS, wide), F32),
        ],
        smem=1,
        count=3 + rows + slots,
        cost=estimate(4 * 4 * pair_work, 4e6, pair_work / HEAD),
    )(info, start_w, place_w, *q_parts, *kv_all)

    x_all = jnp.stack(x_parts)
    g_all = jnp.stack(g_parts)
    out, normed_two, hidden, dgate, dup, dmiddle, do, delta, two, out_grad = feed(
        o, x_all, g_all, gain_b, w_out, w_gate, w_up, w_down
    )
    count = rows * tokens
    flat = lambda value: value.reshape(count, value.shape[-1])
    down_grad = tdot(flat(hidden), flat(g_all)).astype(BF16)
    gate_grad = tdot(flat(normed_two), flat(dgate)).astype(BF16)
    up_grad = tdot(flat(normed_two), flat(dup)).astype(BF16)

    seq_bits = [1 << i for i in range(seq.bit_length() - 1)]
    batch_bits = [("batch", 1 << i) for i in range(batch.bit_length() - 1)]
    near, far = [("seq", seq_bits[0])], [("seq", b) for b in seq_bits[1:]]
    one_way = near + far + batch_bits
    other_way = near + far[::-1] + batch_bits

    def summed(value, steps):
        return gather_back(*scatter_sum(value, steps))

    out_back = back(out)
    down_sum = summed(down_grad, one_way)
    gate_sum = summed(gate_grad, one_way)
    up_sum = summed(up_grad, other_way)

    dq, own, *others = call(
        functools.partial(attend_back_body, parts, rows),
        [
            ((rows, KV_HEADS, HEAD, wide), BF16),
            ((rows, KV_HEADS, tokens, 2 * HEAD), F32),
            *[((rows, KV_HEADS, tokens, 2 * HEAD), BF16)] * (parts - 1),
        ],
        scratch=[
            pltpu.VMEM((slots, KV_HEADS, tokens, HEAD), BF16),
            pltpu.VMEM((slots, KV_HEADS, tokens, HEAD), BF16),
            pltpu.VMEM((slots, KV_HEADS, HEAD, tokens), BF16),
            pltpu.VMEM((KV_HEADS, 2 * wide, 2 * HEAD), BF16),
            pltpu.VMEM((KV_HEADS, HEAD, wide), F32),
            pltpu.VMEM((slots, KV_HEADS, tokens, 2 * HEAD), F32),
        ],
        smem=1,
        count=8 + rows + slots,
        cost=estimate(10 * 4 * pair_work, 8e6, pair_work / HEAD),
    )(info, start_w, place_w, cos_t, sin_t, lse, delta, do, *q_parts, *kv_all)
    got = []
    for i, other in enumerate(others, 1):
        pairs = [
            (r * parts + p, r * parts + (p + i) % parts) for r in range(rows) for p in range(parts)
        ]
        got.append(lax.ppermute(other, "seq", pairs))
    ig, dq_n, dkv_n, normed_one, one = last(
        dq, own, got, x_all, dmiddle, gain_a, wq_t, wkv_t, cos_n, ahead, behind
    )
    ig_back = back(ig)
    query_grad = tdot(flat(normed_one), flat(dq_n)).astype(BF16)
    pair_grad = tdot(flat(normed_one), flat(dkv_n)).astype(BF16)
    tail = jnp.concatenate([out_grad.astype(BF16), query_grad, pair_grad], axis=1)
    tail_sum = summed(tail, one_way).astype(F32)
    gains = jnp.concatenate([one, two], axis=0)
    for axis, bit in one_way:
        gains = gains + swap(gains, axis, bit)
    pair_sum = tail_sum[:, 2 * width :].reshape(width, KV_HEADS, 2, HEAD)
    return (
        place_rows(out_back, BF16),
        place_rows(ig_back, F32),
        gains[0],
        gains[1],
        tail_sum[:, width : 2 * width],
        pair_sum[:, :, 0, :].reshape(width, kv_width),
        pair_sum[:, :, 1, :].reshape(width, kv_width),
        tail_sum[:, :width],
        gate_sum.astype(F32),
        up_sum.astype(F32),
        down_sum.astype(F32),
    )


def solution(mesh):
    tokens_spec = P("batch", "seq", None)
    return jax.shard_map(
        shards,
        mesh=mesh,
        in_specs=(tokens_spec, P("batch", None), *([P()] * 9), tokens_spec),
        out_specs=(tokens_spec, tokens_spec, *([P()] * 9)),
        check_vma=False,
    )
```

```python
import functools
import math

import jax
import jax.numpy as jnp
from jax import lax
from jax.experimental import pallas as pl
from jax.experimental.pallas import tpu as pltpu
from jax.sharding import PartitionSpec as P

HEADS = 9
KV_HEADS = 3
HEAD = 64
GROUPS = HEADS // KV_HEADS
HALF = HEAD // 2
EPSILON = 1e-05
ROPE_BASE = 10000.0
FAR_NEGATIVE = -1e30
SUM_ROWS = 16

F32 = jnp.float32
BF16 = jnp.bfloat16
VMEM_LIMIT = 56 * 1024 * 1024


def rms_factor(values):
    return lax.rsqrt(jnp.mean(values * values, axis=0, keepdims=True) + EPSILON)


def norm_back(source, factor, gain_value, upstream):
    scaled = upstream * gain_value
    return factor * scaled - source * factor * factor * factor * jnp.mean(
        scaled * source, axis=0, keepdims=True
    )


def mdot(left, right):
    return jnp.dot(left, right, preferred_element_type=F32)


def tdot(left, right):
    return lax.dot_general(left, right, (((0,), (0,)), ((), ())), preferred_element_type=F32)


def rdot(left, right):
    return lax.dot_general(left, right, (((1,), (1,)), ((), ())), preferred_element_type=F32)


VM = pl.BlockSpec(memory_space=pltpu.VMEM)
SM = pl.BlockSpec(memory_space=pltpu.SMEM)


def call(body, outs, in_specs, out_specs=None, scratch=(), cost=None, **more):
    return pl.pallas_call(
        body,
        out_shape=[jax.ShapeDtypeStruct(*o) for o in outs],
        in_specs=in_specs,
        out_specs=out_specs or [VM] * len(outs),
        scratch_shapes=list(scratch),
        compiler_params=pltpu.CompilerParams(vmem_limit_bytes=VMEM_LIMIT),
        cost_estimate=cost,
        **more,
    )


def whole(*shape):
    return pl.BlockSpec(shape, lambda *unused: (0,) * len(shape))


def estimate(flops, nbytes, trans=0):
    return pl.CostEstimate(
        flops=int(flops), bytes_accessed=int(nbytes), transcendentals=int(trans)
    )


def pair_body(rows, gain_ref, w_ref, cos_ref, sin_ref, *refs):
    x_refs, (normed_ref, kv_ref) = refs[:rows], refs[rows:]
    for row in range(rows):
        x = x_refs[row][...].astype(F32)
        normed = (x * rms_factor(x) * gain_ref[...]).astype(BF16)
        normed_ref[row] = normed
        turned = mdot(w_ref[...], normed)
        cos, sin = cos_ref[row], sin_ref[row]
        for head in range(KV_HEADS):
            at = head * HEAD
            a, b = turned[at : at + HALF], turned[at + HALF : at + HEAD]
            kv_ref[row, head, :HALF, :] = (a * cos - b * sin).astype(BF16)
            kv_ref[row, head, HALF:HEAD, :] = (b * cos + a * sin).astype(BF16)
            at += KV_HEADS * HEAD
            kv_ref[row, head, HEAD:, :] = turned[at : at + HEAD].astype(BF16)


def query_body(rows, normed_ref, w_ref, cos_ref, sin_ref, q_ref):
    tokens = normed_ref.shape[-1]
    for row in range(rows):
        turned = mdot(w_ref[...], normed_ref[row])
        cos, sin = cos_ref[row] * 0.125, sin_ref[row] * 0.125
        for head in range(HEADS):
            a = turned[head * HEAD : head * HEAD + HALF]
            b = turned[head * HEAD + HALF : (head + 1) * HEAD]
            kv, lane = head // GROUPS, (head % GROUPS) * tokens
            q_ref[row, kv, :HALF, lane : lane + tokens] = (a * cos - b * sin).astype(BF16)
            q_ref[row, kv, HALF:, lane : lane + tokens] = (b * cos + a * sin).astype(BF16)


def owner(block, parts):
    group, place = block // parts, block % parts
    return jnp.where(group % 2 == 0, place, parts - 1 - place)


def slot_of(block, info, parts, rows):
    relative = (owner(block, parts) - info[1] + parts) % parts
    return relative * rows + ((block // parts) ^ info[0])


def visible(block, start, place, shape):
    key_place = block * shape[0] + lax.broadcasted_iota(jnp.int32, shape, 0)
    return (key_place >= start) & (key_place <= place)


def attend_body(parts, rows, info_ref, start_ref, place_ref, q_ref, *refs):
    kv_refs, refs = refs[:parts], refs[parts:]
    o_ref, lse_ref, k_nat, v_aug, acc = refs
    tokens = kv_refs[0].shape[-1]
    info = (info_ref[0], info_ref[1])
    ones = (lax.broadcasted_iota(jnp.int32, (SUM_ROWS, tokens), 0) == 0).astype(BF16)
    for slot in range(rows * parts):
        kv_ref = kv_refs[slot // rows].at[slot % rows]
        for head in range(KV_HEADS):
            k_nat[slot, head] = kv_ref[head, :HEAD, :].T
            v_aug[slot, head, :HEAD, :] = kv_ref[head, HEAD:, :]
            v_aug[slot, head, HEAD:, :] = ones

    for row in range(rows):
        mine, low, full = info_ref[2 + 3 * row], info_ref[3 + 3 * row], info_ref[4 + 3 * row]
        acc[...] = jnp.zeros_like(acc)
        start, place = start_ref[row], place_ref[row]

        def step(block, tops, masked):
            slot = slot_of(block, info, parts, rows)
            allowed = visible(block, start, place, (tokens, start.shape[-1])) if masked else None
            result = []
            for head in range(KV_HEADS):
                scores = mdot(k_nat[slot, head], q_ref[row, head])
                if masked:
                    scores = jnp.where(allowed, scores, FAR_NEGATIVE)
                top = jnp.maximum(tops[head], jnp.max(scores, axis=0, keepdims=True))
                weights = jnp.exp(scores - top).astype(BF16)
                acc[head] = acc[head] * jnp.exp(tops[head] - top) + mdot(v_aug[slot, head], weights)
                result.append(top)
            return tuple(result)

        tops = tuple(
            jnp.full((1, start.shape[-1]), FAR_NEGATIVE, F32) for unused in range(KV_HEADS)
        )
        middle = jnp.minimum(full, mine)
        tops = lax.fori_loop(low, middle, lambda b, s: step(b, s, True), tops)
        tops = lax.fori_loop(middle, mine, lambda b, s: step(b, s, False), tops)
        tops = step(mine, tops, True)
        for head in range(KV_HEADS):
            mass = acc[head, HEAD : HEAD + 1, :]
            o_ref[row, head] = (acc[head, :HEAD, :] / mass).astype(BF16)
            lse_ref[row, head] = tops[head] + jnp.log(mass)


def attend_back_body(parts, rows, info_ref, start_ref, place_ref, cos_ref, sin_ref, lse_ref, delta_ref, do_ref, q_ref, *refs):
    kv_refs, refs = refs[:parts], refs[parts:]
    dq_ref, own_ref = refs[:2]
    other_refs = refs[2 : 1 + parts]
    k_nat, v_nat, pair, dq_acc, dkv = refs[1 + parts :]
    tokens = kv_refs[0].shape[-1]
    wide = GROUPS * tokens
    info = (info_ref[0], info_ref[1])
    for slot in range(rows * parts):
        k_nat[slot] = kv_refs[slot // rows][slot % rows, 0, :HEAD, :].T
        v_nat[slot] = kv_refs[slot // rows][slot % rows, 0, HEAD:, :].T
    dkv[...] = jnp.zeros_like(dkv)
    blank = jnp.zeros((wide, HEAD), BF16)

    for row in range(rows):
        mine, low, full = info_ref[2 + 3 * row], info_ref[3 + 3 * row], info_ref[4 + 3 * row]
        dq_acc[...] = jnp.zeros_like(dq_acc)
        start, place = start_ref[row], place_ref[row]
        pair[:wide, :] = jnp.concatenate([q_ref[row, 0].T, blank], axis=1)
        pair[wide:, :] = jnp.concatenate([blank, do_ref[row, 0].T], axis=1)

        def step(block, masked):
            slot = slot_of(block, info, parts, rows)
            scores = mdot(k_nat[slot], q_ref[row, 0])
            back = mdot(v_nat[slot], do_ref[row, 0])
            weights = jnp.exp(scores - lse_ref[row, 0])
            if masked:
                allowed = visible(block, start, place, (tokens, wide))
                weights = jnp.where(allowed, weights, 0.0)
            slope = (weights * (back - delta_ref[row, 0])).astype(BF16)
            both = jnp.concatenate([slope, weights.astype(BF16)], axis=1)
            dkv[slot] += mdot(both, pair[...])
            return slope, slot

        def masked_step(block, carry):
            slope, slot = step(block, True)
            dq_acc[...] += mdot(k_nat[slot].T, slope)
            return carry

        def two_steps(index, carry):
            block = middle + 2 * index
            one, slot_one = step(block, False)
            two, slot_two = step(block + 1, False)
            turned = jnp.concatenate([k_nat[slot_one].T, k_nat[slot_two].T], axis=1)
            dq_acc[...] += mdot(turned, jnp.concatenate([one, two], axis=0))
            return carry

        middle = jnp.minimum(full, mine)
        count = mine - middle
        lax.fori_loop(low, middle, masked_step, 0)
        lax.fori_loop(0, count // 2, two_steps, 0)

        @pl.when(count % 2 == 1)
        def _():
            slope, slot = step(mine - 1, False)
            dq_acc[...] += mdot(k_nat[slot].T, slope)

        masked_step(mine, 0)
        cos, sin = cos_ref[row], sin_ref[row]
        for group in range(GROUPS):
            lanes = slice(group * tokens, (group + 1) * tokens)
            a = dq_acc[:HALF, lanes] * 0.125
            b = dq_acc[HALF:, lanes] * 0.125
            dq_ref[row, group * HEAD : group * HEAD + HALF, :] = (a * cos + b * sin).astype(BF16)
            dq_ref[row, group * HEAD + HALF : (group + 1) * HEAD, :] = (b * cos - a * sin).astype(BF16)
    own_ref[...] = dkv[:rows]
    for i, other_ref in enumerate(other_refs):
        other_ref[...] = dkv[(i + 1) * rows : (i + 2) * rows].astype(BF16)


def keep_and_send(core, first, second):
    return jnp.where(core == 0, first, second), jnp.where(core == 0, second, first)


def middle_body(rows, o_ref, gain_ref, wo_ref, *refs):
    x_refs, g_refs = refs[:rows], refs[rows : 2 * rows]
    attended, grad, middle, normed = refs[2 * rows :]
    tokens = x_refs[0].shape[1]
    for row in range(rows):
        lanes = slice(row * tokens, (row + 1) * tokens)
        grad[:, lanes] = g_refs[row][...]
        for head in range(HEADS):
            lane = (head % GROUPS) * tokens
            attended[head * HEAD : (head + 1) * HEAD, lanes] = o_ref[
                row, head // GROUPS, :, lane : lane + tokens
            ]
    turned = wo_ref[...].T
    for row in range(rows):
        lanes = slice(row * tokens, (row + 1) * tokens)
        total = x_refs[row][...].astype(F32) + mdot(turned, attended[:, lanes])
        middle[:, lanes] = total
        normed[:, lanes] = (total * rms_factor(total) * gain_ref[...]).astype(BF16)


def feed_body(core_ref, normed, grad, wg_ref, wu_ref, wd_ref, keep_ref, send_ref, hid_ref, dgate_ref, dup_ref):
    gate = mdot(wg_ref[...].T, normed[...])
    up = mdot(wu_ref[...].T, normed[...])
    sig = jax.nn.sigmoid(gate)
    silu = gate * sig
    hidden = (silu * up).astype(BF16)
    dhidden = mdot(wd_ref[...].T, grad[...])
    dgate = (dhidden * up * sig * (1.0 + gate * (1.0 - sig))).astype(BF16)
    dup = (dhidden * silu).astype(BF16)
    hid_ref[...] = hidden
    dgate_ref[...] = dgate
    dup_ref[...] = dup
    half = keep_ref.shape[0] // 3
    sums = (rdot(normed[...], dgate), rdot(normed[...], dup), rdot(grad[...], hidden))
    for i, value in enumerate(sums):
        value = value.astype(BF16)
        span = slice(i * half, (i + 1) * half)
        keep_ref[span], send_ref[span] = keep_and_send(core_ref[0], value[:half], value[half:])


def out_body(rows, middle, wd_ref, hid_ref, *out_refs):
    tokens = out_refs[0].shape[1]
    for row in range(rows):
        lanes = slice(row * tokens, (row + 1) * tokens)
        out_refs[row][...] = (middle[:, lanes] + mdot(wd_ref[...], hid_ref[:, lanes])).astype(BF16)


def turn_body(rows, attended, grad, middle, gain_ref, wo_ref, wg_ref, wu_ref, dgate_ref, dup_ref, *refs):
    og_ref, dmid_ref, do_ref, delta_ref, two_ref, branches = refs
    tokens = dmid_ref.shape[-1]
    gain = gain_ref[...]
    two = jnp.zeros(two_ref.shape, F32)
    for row in range(rows):
        lanes = slice(row * tokens, (row + 1) * tokens)
        source = middle[:, lanes]
        dnormed = mdot(wg_ref[...], dgate_ref[:, lanes]) + mdot(wu_ref[...], dup_ref[:, lanes])
        scale = rms_factor(source)
        two = two + jnp.sum(dnormed * source * scale, axis=1, keepdims=True)
        dmiddle = grad[:, lanes].astype(F32) + norm_back(source, scale, gain, dnormed)
        dmid_ref[row] = dmiddle
        branch = dmiddle.astype(BF16)
        branches[:, lanes] = branch
        dattended = mdot(wo_ref[...], branch).astype(BF16)
        product = dattended.astype(F32) * attended[:, lanes].astype(F32)
        for head in range(HEADS):
            kv, lane = head // GROUPS, (head % GROUPS) * tokens
            span = slice(head * HEAD, (head + 1) * HEAD)
            do_ref[row, kv, :, lane : lane + tokens] = dattended[span]
            delta_ref[row, kv, :, lane : lane + tokens] = jnp.sum(
                product[span], axis=0, keepdims=True
            )
    two_ref[...] = two
    og_ref[...] = rdot(attended[...], branches[...]).astype(BF16)


def last_body(rows, parts, core_ref, dmid_ref, gain_ref, wq_ref, wkv_ref, cos_ref, sin_ref, og_ref, two_ref, normed_ref, *refs):
    x_refs, refs = refs[:rows], refs[rows:]
    dq_refs, refs = refs[:KV_HEADS], refs[KV_HEADS:]
    own_refs, refs = refs[:KV_HEADS], refs[KV_HEADS:]
    other_refs, refs = refs[: KV_HEADS * (parts - 1)], refs[KV_HEADS * (parts - 1) :]
    ig_refs, refs = refs[:rows], refs[rows:]
    keep_ref, send_ref, normed, dall = refs
    width, tokens = x_refs[0].shape
    kv_width = KV_HEADS * HEAD
    gain = gain_ref[...]
    one = jnp.zeros(gain_ref.shape, F32)
    for row in range(rows):
        lanes = slice(row * tokens, (row + 1) * tokens)
        x = x_refs[row][...].astype(F32)
        factor = rms_factor(x)
        normed[:, lanes] = normed_ref[row]
        cos, sin = cos_ref[row], sin_ref[row]
        for head in range(KV_HEADS):
            dall[head * kv_width : (head + 1) * kv_width, lanes] = dq_refs[head][row]
            total = own_refs[head][row]
            for i in range(parts - 1):
                total = total + other_refs[head * (parts - 1) + i][row].astype(F32)
            turned = total.T
            a, b = turned[:HALF], turned[HALF:HEAD]
            at = width + head * HEAD
            dall[at : at + HALF, lanes] = (a * cos + b * sin).astype(BF16)
            dall[at + HALF : at + HEAD, lanes] = (b * cos - a * sin).astype(BF16)
            at += kv_width
            dall[at : at + HEAD, lanes] = turned[HEAD:].astype(BF16)
        dnormed = mdot(wq_ref[...], dall[:width, lanes]) + mdot(wkv_ref[...], dall[width:, lanes])
        one = one + jnp.sum(dnormed * x * factor, axis=1, keepdims=True)
        ig_refs[row][...] = (dmid_ref[row] + norm_back(x, factor, gain, dnormed)).astype(BF16)
    query = rdot(normed[...], dall[:width]).astype(BF16)
    pair = rdot(dall[width:], normed[...]).astype(BF16)
    core = core_ref[0]
    half = keep_ref.shape[0]
    cut = half - width
    spare = keep_ref.shape[1] - width
    lane = lax.broadcasted_iota(jnp.int32, (width, spare), 1)
    gains = jnp.where(lane == 0, one, jnp.where(lane == 1, two_ref[...], 0.0)).astype(BF16)
    blank = jnp.zeros((half, spare), BF16)
    low = jnp.concatenate([og_ref[...], query[:cut]], axis=0)
    low = jnp.concatenate([low, jnp.concatenate([gains, blank[:cut]], axis=0)], axis=1)
    high = jnp.concatenate([query[cut:], pair], axis=0)
    high = jnp.concatenate([high, blank], axis=1)
    keep_ref[...], send_ref[...] = keep_and_send(core, low, high)


def bit_length(size):
    return [1 << i for i in range(size.bit_length() - 1)]


def swap(value, axis, bit):
    size = lax.axis_size(axis)
    return lax.ppermute(value, axis, [(i, i ^ bit) for i in range(size)])


def pick(value, index):
    return lax.dynamic_index_in_dim(value, index, 0, keepdims=False)


def after(value, *others):
    return lax.optimization_barrier((value, *others))[0]


def join(*trees):
    return lax.optimization_barrier(trees)


def place_body(count, copies, mine_ref, *refs):
    out_ref = refs[count]
    for k in range(count):
        value = refs[k][...].astype(out_ref.dtype)
        for i in range(copies):
            out_ref[i, mine_ref[0] ^ k] = value


def placed(pieces, mine, dtype=BF16, copies=1):
    count = len(pieces)
    return call(
        functools.partial(place_body, count, copies),
        [((copies, count, *pieces[0].shape), dtype)],
        [SM] + [VM] * count,
        cost=estimate(0, 2 * (1 + copies) * count * pieces[0].size),
    )(mine.reshape(1), *pieces)[0]


def unpack_body(core_ref, mine_ref, other_ref, *out_refs):
    outer, inner = mine_ref.shape[:2]
    half = out_refs[0].shape[0] // 2
    for ref, core in ((mine_ref, core_ref[0]), (other_ref, 1 - core_ref[0])):
        value = jnp.concatenate(
            [jnp.concatenate([ref[i, j] for j in range(inner)], axis=1) for i in range(outer)],
            axis=0,
        ).astype(F32)
        for i, out_ref in enumerate(out_refs):
            rows = pl.ds(pl.multiple_of(core * half, half), half)
            out_ref[rows, :] = value[i * half : (i + 1) * half]


def unpack(core, mine, other, width, hidden):
    outer, inner, rows, lanes = mine.shape
    each = 1 if lanes % 128 == 0 else 2
    block = pl.BlockSpec((outer, each, rows, lanes), lambda i: (0, i, 0, 0))
    return call(
        unpack_body,
        [((width, hidden), F32)] * 3,
        [SM, block, block],
        [pl.BlockSpec((width, each * lanes), lambda i: (0, i))] * 3,
        grid=(inner // each,),
        cost=estimate(0, 18 * width * hidden),
    )(core, mine, other)


def tail_body(core_ref, mine_ref, other_ref, o_ref, q_ref, k_ref, v_ref, gain_ref):
    width, kv = o_ref.shape[1], k_ref.shape[0]
    even = core_ref[0] == 0
    low = jnp.where(even, mine_ref[...], other_ref[...]).astype(F32)
    high = jnp.where(even, other_ref[...], mine_ref[...]).astype(F32)
    cut = low.shape[0] - width
    o_ref[...] = low[:width, :width]
    gain_ref[...] = low[:width, width:]
    q_ref[:cut] = low[width:, :width]
    q_ref[cut:] = high[: width - cut, :width]
    k_ref[...] = high[width - cut : width - cut + kv, :width]
    v_ref[...] = high[width - cut + kv :, :width]


class Axis:
    def __init__(self, name, bit):
        self.name, self.bit = name, bit
        self.size = lax.axis_size(name) // bit
        self.mine = lax.axis_index(name) // bit
        self.groups = None
        if bit > 1:
            self.groups = [[c + bit * i for i in range(self.size)] for c in range(bit)]

    def trade(self, value):
        return lax.all_to_all(value, self.name, 0, 0, tiled=True, axis_index_groups=self.groups)

    def spread(self, value):
        return self.trade(jnp.broadcast_to(value, (self.size, *value.shape)))

    def send_parts(self, value):
        return [pick(value, self.mine)] + [
            swap(pick(value, self.mine ^ k), self.name, k * self.bit)
            for k in range(1, self.size)
        ]

    def send_all(self, value):
        return [value] + [swap(value, self.name, k * self.bit) for k in range(1, self.size)]


def total(pieces):
    result = pieces[0].astype(F32)
    for piece in pieces[1:]:
        result = result + piece.astype(F32)
    return result.astype(BF16)


def folded(value):
    return jnp.sum(value.astype(F32), axis=0).astype(BF16)


def split_columns(value, size):
    return jnp.swapaxes(value.reshape(value.shape[0], size, -1), 0, 1)


def shards(
    inputs, doc_lengths, gain_one, gain_two, w_query, w_key, w_value, w_out, w_gate, w_up, w_down, cotangent
):
    rows, tokens, width = inputs.shape
    hidden = w_gate.shape[1]
    seq = lax.axis_size("seq")
    batch = lax.axis_size("batch")
    parts = seq // rows
    me = lax.axis_index("seq")
    group, part = me // parts, me % parts
    wide = GROUPS * tokens
    kv_width = KV_HEADS * HEAD

    def dealt(block):
        g, place = block // parts, block % parts
        return g, place if g % 2 == 0 else parts - 1 - place

    def route(step):
        pairs = []
        for block in range(seq):
            g, p = dealt(block)
            pairs.append((block, (g ^ step) * parts + p))
        return pairs

    def bring(value):
        return [lax.ppermute(pick(value, group ^ step), "seq", route(step)) for step in range(rows)]

    def back(pieces):
        return [
            lax.ppermute(piece, "seq", [(b, a) for a, b in route(step)])
            for step, piece in enumerate(pieces)
        ]

    def place_rows(pieces, dtype):
        return jnp.swapaxes(placed(pieces, group, dtype)[0], 1, 2)

    x_parts = bring(jnp.swapaxes(inputs, 1, 2))
    held = lax.optimization_barrier((cotangent, *x_parts))
    x_parts = list(held[1:])
    g_parts = bring(jnp.swapaxes(held[0], 1, 2))

    groups_here = group ^ jnp.arange(rows, dtype=jnp.int32)
    blocks = groups_here * parts + jnp.where(groups_here % 2 == 0, part, parts - 1 - part)
    lengths = pick(doc_lengths, group)
    order = jnp.arange(lengths.shape[0])
    ends = jnp.sum(jnp.where(order[None, :] <= order[:, None], lengths[None, :], 0), axis=1)
    places = blocks[:, None] * tokens + jnp.arange(tokens, dtype=jnp.int32)[None, :]
    starts = jnp.sum(jnp.where(ends <= places[..., None], lengths, 0), axis=-1)
    info = jnp.concatenate(
        [
            jnp.stack([group, part]),
            jnp.stack(
                [blocks, starts[:, 0] // tokens, (starts[:, -1] + tokens - 1) // tokens], axis=1
            ).reshape(-1),
        ]
    ).astype(jnp.int32)
    inverse = 1.0 / ROPE_BASE ** (jnp.arange(HALF, dtype=F32) * (2.0 / HEAD))
    angles = (places - starts).astype(F32)[:, None, :] * inverse[None, :, None]
    cos_t, sin_t = jnp.cos(angles), jnp.sin(angles)
    start_w = jnp.tile(starts[:, None, :], (1, 1, GROUPS))
    place_w = jnp.tile(places[:, None, :], (1, 1, GROUPS))
    gain_a = gain_one.astype(F32)[:, None]
    gain_b = gain_two.astype(F32)[:, None]
    w_pair = jnp.concatenate([w_key, w_value], axis=1)
    core = (me % 2).reshape(1)

    normed, kv = call(
        functools.partial(pair_body, rows),
        [((rows, width, tokens), BF16), ((rows, KV_HEADS, 2 * HEAD, tokens), BF16)],
        [VM] * (4 + rows),
        cost=estimate(4 * rows * tokens * width * kv_width, 3e6),
    )(gain_a, w_pair.T, cos_t, sin_t, *x_parts)

    def ring(i, value):
        pairs = [
            (r * parts + (p + i) % parts, r * parts + p) for r in range(rows) for p in range(parts)
        ]
        return lax.ppermute(value, "seq", pairs)

    kv_all = [kv] + [ring(i, kv) for i in range(1, parts)]
    q = call(
        functools.partial(query_body, rows),
        [((rows, KV_HEADS, HEAD, wide), BF16)],
        [VM] * 4,
        cost=estimate(2 * rows * tokens * width * width, 3e6),
    )(normed, w_query.T, cos_t, sin_t)[0]
    q, kv_all = join(q, kv_all)

    slots = rows * parts
    pair_work = rows * (seq + 1) / 2 * tokens * tokens * HEADS * HEAD
    o, lse = call(
        functools.partial(attend_body, parts, rows),
        [((rows, KV_HEADS, HEAD, wide), BF16), ((rows, KV_HEADS, 1, wide), F32)],
        [SM] + [VM] * (3 + parts),
        scratch=[
            pltpu.VMEM((slots, KV_HEADS, tokens, HEAD), BF16),
            pltpu.VMEM((slots, KV_HEADS, HEAD + SUM_ROWS, tokens), BF16),
            pltpu.VMEM((KV_HEADS, HEAD + SUM_ROWS, wide), F32),
        ],
        cost=estimate(4 * 4 * pair_work, 4e6, pair_work / HEAD),
    )(info, start_w, place_w, q, *kv_all)
    o, g_parts = join(o, g_parts)

    plane, line = Axis("seq", 2), Axis("batch", 1)
    count = rows * tokens
    chunks = 3
    chunk = hidden // chunks
    w_down_t = w_down.T
    attended, grad, middle, normed_two = call(
        functools.partial(middle_body, rows),
        [((width, count), BF16), ((width, count), BF16), ((width, count), F32), ((width, count), BF16)],
        [VM] * (3 + 2 * rows),
        cost=estimate(2 * count * width * width, 1.2e7),
    )(o, gain_b, w_out, *x_parts, *g_parts)

    columns = pl.BlockSpec((width, chunk), lambda i: (0, i))
    rows_of = pl.BlockSpec((chunk, count), lambda i: (i, 0))
    keep, send, hid, dgate, dup = call(
        feed_body,
        [*[((3 * width // 2, hidden), BF16)] * 2, *[((hidden, count), BF16)] * 3],
        [SM, whole(width, count), whole(width, count), columns, columns, columns],
        [*[pl.BlockSpec((3 * width // 2, chunk), lambda i: (0, i))] * 2, *[rows_of] * 3],
        grid=(chunks,),
        cost=estimate(2 * count * 6 * width * hidden, 2e7, count * hidden),
    )(core, normed_two, grad, w_gate, w_up, w_down_t)
    got = swap(send, "seq", 1)
    out = call(
        functools.partial(out_body, rows),
        [((width, tokens), BF16)] * rows,
        [VM] * 3,
        cost=estimate(2 * count * width * hidden, 8e6),
    )(middle, w_down_t, hid)
    got, out, dgate = join(got, out, dgate)
    part = total([keep, got]).reshape(plane.size, -1, hidden)
    part, dgate = join(part, dgate)
    trade = plane.trade(part)
    og, dmiddle, do, delta, two = call(
        functools.partial(turn_body, rows),
        [
            ((width, width), BF16),
            ((rows, width, tokens), F32),
            ((rows, KV_HEADS, HEAD, wide), BF16),
            ((rows, KV_HEADS, 1, wide), F32),
            ((width, 1), F32),
        ],
        [VM] * 9,
        scratch=[pltpu.VMEM((width, count), BF16)],
        cost=estimate(2 * count * width * (2 * hidden + 2 * width), 2.5e7),
    )(attended, grad, middle, gain_b, w_out, w_gate, w_up, dgate, dup)

    def back_call(head, do):
        one_head = lambda *shape: pl.BlockSpec(
            (rows, 1, *shape), lambda i: (0, head) + (0,) * len(shape)
        )
        return call(
            functools.partial(attend_back_body, parts, rows),
            [
                ((rows, GROUPS * HEAD, tokens), BF16),
                ((rows, tokens, 2 * HEAD), F32),
                *[((rows, tokens, 2 * HEAD), BF16)] * (parts - 1),
            ],
            [
                SM, whole(rows, 1, wide), whole(rows, 1, wide), whole(rows, HALF, tokens),
                whole(rows, HALF, tokens), one_head(1, wide), one_head(1, wide),
                one_head(HEAD, wide), one_head(HEAD, wide), *[one_head(2 * HEAD, tokens)] * parts,
            ],
            [whole(rows, GROUPS * HEAD, tokens)] + [whole(rows, tokens, 2 * HEAD)] * parts,
            scratch=[
                pltpu.VMEM((slots, tokens, HEAD), BF16),
                pltpu.VMEM((slots, tokens, HEAD), BF16),
                pltpu.VMEM((2 * wide, 2 * HEAD), BF16),
                pltpu.VMEM((HEAD, wide), F32),
                pltpu.VMEM((slots, tokens, 2 * HEAD), F32),
            ],
            grid=(1,),
            cost=estimate(10 * 4 * pair_work / KV_HEADS, 3e6, pair_work / HEAD / KV_HEADS),
        )(info, start_w, place_w, cos_t, sin_t, lse, delta, do, q, *kv_all)

    def deliver(others):
        got = []
        for i, other in enumerate(others, 1):
            pairs = [
                (r * parts + p, r * parts + (p + i) % parts)
                for r in range(rows)
                for p in range(parts)
            ]
            got.append(lax.ppermute(other, "seq", pairs))
        return got

    dq0, own0, *others0 = back_call(0, do)
    got0 = deliver(others0)
    dq0, do = join(dq0, do)
    dq1, own1, *others1 = back_call(1, do)
    trade, dq1, own1, others1, got0, do, out = join(trade, dq1, own1, others1, got0, do, out)
    part = split_columns(folded(trade), batch)
    part, do, out, others1 = join(part, do, out, others1)
    got1 = deliver(others1)
    pieces = line.send_parts(part)
    out_back = back(out)
    dq2, own2, *others2 = back_call(2, do)
    pieces, dq2, own2, others2 = join(pieces, dq2, own2, others2)
    part = total(pieces)
    part, dq2, others2 = join(part, dq2, others2)
    got2 = deliver(others2)
    pieces = line.send_all(part)
    lanes = -(-width // 128) * 128
    *ig, keep, send = call(
        functools.partial(last_body, rows, parts),
        [*[((width, tokens), BF16)] * rows, *[((width + kv_width, lanes), BF16)] * 2],
        [SM] + [VM] * (9 + rows + KV_HEADS * (1 + parts)),
        scratch=[
            pltpu.VMEM((width, count), BF16),
            pltpu.VMEM((width + 2 * kv_width, count), BF16),
        ],
        cost=estimate(4 * rows * tokens * 5.6e5, 1.2e7),
    )(
        core, dmiddle, gain_a, w_query, w_pair, cos_t, sin_t, og, two, normed, *x_parts,
        dq0, dq1, dq2, own0, own1, own2, *got0, *got1, *got2,
    )
    send, keep, ig, out_back = join(send, keep, ig, out_back)
    got = swap(send, "seq", 1)
    output = place_rows(out_back, BF16)
    got, keep, ig, output = join(got, keep, ig, output)
    tail = total([keep, got]).reshape(plane.size, -1, lanes)
    tail, ig = join(tail, ig)
    trade = plane.trade(tail)
    ig_back = back(ig)
    part = placed(pieces, line.mine, copies=plane.size)
    trade, part = join(trade, part)
    tail = folded(trade).reshape(batch, -1, lanes)
    tail, part = join(tail, part)
    tail_pieces = line.send_parts(tail)
    feed_all = plane.trade(part)
    tail_pieces = line.send_all(total(tail_pieces))
    tail = placed(tail_pieces, line.mine)[0].reshape(-1, lanes)
    tail_pieces = plane.send_all(tail)
    tail_all = placed(tail_pieces, plane.mine)[0].reshape(-1, lanes)
    tail_other = swap(tail_all, "seq", 1)
    input_grad = place_rows(ig_back, F32)
    feed_all, tail_other, input_grad = join(feed_all, tail_other, input_grad)
    feed_other = swap(feed_all, "seq", 1)
    w_gate_sum, w_up_sum, w_down_sum = unpack(core, feed_all, feed_other, width, hidden)
    w_out_sum, w_query_sum, w_key_sum, w_value_sum, gains = call(
        tail_body,
        [
            *[((width, width), F32)] * 2,
            *[((kv_width, width), F32)] * 2,
            ((width, lanes - width), F32),
        ],
        [SM, VM, VM],
        cost=estimate(0, 6e6),
    )(core, tail_all, tail_other)
    return (
        output,
        input_grad,
        gains[:, 0],
        gains[:, 1],
        w_query_sum,
        w_key_sum.T,
        w_value_sum.T,
        w_out_sum,
        w_gate_sum,
        w_up_sum,
        w_down_sum.T,
    )


def solution(mesh):
    tokens_spec = P("batch", "seq", None)
    return jax.shard_map(
        shards,
        mesh=mesh,
        in_specs=(tokens_spec, P("batch", None), *([P()] * 9), tokens_spec),
        out_specs=(tokens_spec, tokens_spec, *([P()] * 9)),
        check_vma=False,
    )
```

```python
import functools
import math

import jax
import jax.numpy as jnp
from jax import lax
from jax.experimental import pallas as pl
from jax.experimental.pallas import tpu as pltpu
from jax.sharding import PartitionSpec as P

HEADS = 9
KV_HEADS = 3
HEAD = 64
GROUPS = HEADS // KV_HEADS
HALF = HEAD // 2
EPSILON = 1e-05
ROPE_BASE = 10000.0
FAR_NEGATIVE = -1e30
SUM_ROWS = 16

F32 = jnp.float32
BF16 = jnp.bfloat16
VMEM_LIMIT = 56 * 1024 * 1024


def rms_factor(values):
    return lax.rsqrt(jnp.mean(values * values, axis=0, keepdims=True) + EPSILON)


def norm_back(source, factor, gain_value, upstream):
    scaled = upstream * gain_value
    return factor * scaled - source * factor * factor * factor * jnp.mean(
        scaled * source, axis=0, keepdims=True
    )


def mdot(left, right):
    return jnp.dot(left, right, preferred_element_type=F32)


def tdot(left, right):
    return lax.dot_general(left, right, (((0,), (0,)), ((), ())), preferred_element_type=F32)


def rdot(left, right):
    return lax.dot_general(left, right, (((1,), (1,)), ((), ())), preferred_element_type=F32)


VM = pl.BlockSpec(memory_space=pltpu.VMEM)
SM = pl.BlockSpec(memory_space=pltpu.SMEM)


def call(body, outs, in_specs, out_specs=None, scratch=(), cost=None, **more):
    return pl.pallas_call(
        body,
        out_shape=[jax.ShapeDtypeStruct(*o) for o in outs],
        in_specs=in_specs,
        out_specs=out_specs or [VM] * len(outs),
        scratch_shapes=list(scratch),
        compiler_params=pltpu.CompilerParams(vmem_limit_bytes=VMEM_LIMIT),
        cost_estimate=cost,
        **more,
    )


def whole(*shape):
    return pl.BlockSpec(shape, lambda *unused: (0,) * len(shape))


def estimate(flops, nbytes, trans=0):
    return pl.CostEstimate(
        flops=int(flops), bytes_accessed=int(nbytes), transcendentals=int(trans)
    )


def pair_body(rows, gain_ref, wk_ref, wv_ref, cos_ref, sin_ref, *refs):
    gain = column(gain_ref)
    weights = jnp.concatenate([wk_ref[...], wv_ref[...]], axis=0)
    x_refs, (x_all, normed_ref, kv_ref) = refs[:rows], refs[rows:]
    for row in range(rows):
        x_all[row] = x_refs[row][...]
        x = x_refs[row][...].astype(F32)
        normed = (x * rms_factor(x) * gain).astype(BF16)
        normed_ref[row] = normed
        turned = mdot(weights, normed)
        cos, sin = cos_ref[row], sin_ref[row]
        for head in range(KV_HEADS):
            at = head * HEAD
            a, b = turned[at : at + HALF], turned[at + HALF : at + HEAD]
            kv_ref[row, head, :HALF, :] = (a * cos - b * sin).astype(BF16)
            kv_ref[row, head, HALF:HEAD, :] = (b * cos + a * sin).astype(BF16)
            at += KV_HEADS * HEAD
            kv_ref[row, head, HEAD:, :] = turned[at : at + HEAD].astype(BF16)


def query_body(rows, normed_ref, w_ref, cos_ref, sin_ref, q_ref):
    tokens = normed_ref.shape[-1]
    for row in range(rows):
        turned = mdot(w_ref[...], normed_ref[row])
        cos, sin = cos_ref[row] * 0.125, sin_ref[row] * 0.125
        for head in range(HEADS):
            a = turned[head * HEAD : head * HEAD + HALF]
            b = turned[head * HEAD + HALF : (head + 1) * HEAD]
            kv, lane = head // GROUPS, (head % GROUPS) * tokens
            q_ref[row, kv, :HALF, lane : lane + tokens] = (a * cos - b * sin).astype(BF16)
            q_ref[row, kv, HALF:, lane : lane + tokens] = (b * cos + a * sin).astype(BF16)


def owner(block, parts):
    group, place = block // parts, block % parts
    return jnp.where(group % 2 == 0, place, parts - 1 - place)


def slot_of(block, info, parts, rows):
    relative = (owner(block, parts) - info[1] + parts) % parts
    return relative * rows + ((block // parts) ^ info[0])


def spans_of(starts_ref, row, mine):
    start = jnp.concatenate([starts_ref[row : row + 1, :]] * GROUPS, axis=1)
    tokens = starts_ref.shape[1]
    lane = lax.broadcasted_iota(jnp.int32, start.shape, 1)
    return start, mine * tokens + lane % tokens


def visible(block, start, place, shape):
    key_place = block * shape[0] + lax.broadcasted_iota(jnp.int32, shape, 0)
    return (key_place >= start) & (key_place <= place)


def attend_body(parts, rows, info_ref, start_ref, q_ref, *refs):
    kv_refs, refs = refs[:parts], refs[parts:]
    o_ref, lse_ref, k_nat, v_aug, acc = refs
    tokens = kv_refs[0].shape[-1]
    info = (info_ref[0], info_ref[1])
    ones = (lax.broadcasted_iota(jnp.int32, (SUM_ROWS, tokens), 0) == 0).astype(BF16)
    for slot in range(rows * parts):
        kv_ref = kv_refs[slot // rows].at[slot % rows]
        for head in range(KV_HEADS):
            k_nat[slot, head] = kv_ref[head, :HEAD, :].T
            v_aug[slot, head, :HEAD, :] = kv_ref[head, HEAD:, :]
            v_aug[slot, head, HEAD:, :] = ones

    for row in range(rows):
        mine, low, full = info_ref[2 + 3 * row], info_ref[3 + 3 * row], info_ref[4 + 3 * row]
        acc[...] = jnp.zeros_like(acc)
        start, place = spans_of(start_ref, row, mine)

        def step(block, tops, masked):
            slot = slot_of(block, info, parts, rows)
            allowed = visible(block, start, place, (tokens, start.shape[-1])) if masked else None
            result = []
            for head in range(KV_HEADS):
                scores = mdot(k_nat[slot, head], q_ref[row, head])
                if masked:
                    scores = jnp.where(allowed, scores, FAR_NEGATIVE)
                top = jnp.maximum(tops[head], jnp.max(scores, axis=0, keepdims=True))
                weights = jnp.exp(scores - top).astype(BF16)
                acc[head] = acc[head] * jnp.exp(tops[head] - top) + mdot(v_aug[slot, head], weights)
                result.append(top)
            return tuple(result)

        tops = tuple(
            jnp.full((1, start.shape[-1]), FAR_NEGATIVE, F32) for unused in range(KV_HEADS)
        )
        middle = jnp.minimum(full, mine)
        tops = lax.fori_loop(low, middle, lambda b, s: step(b, s, True), tops)
        tops = lax.fori_loop(middle, mine, lambda b, s: step(b, s, False), tops)
        tops = step(mine, tops, True)
        for head in range(KV_HEADS):
            mass = acc[head, HEAD : HEAD + 1, :]
            o_ref[row, head] = (acc[head, :HEAD, :] / mass).astype(BF16)
            lse_ref[row, head] = tops[head] + jnp.log(mass)


def attend_back_body(parts, rows, info_ref, start_ref, cos_ref, sin_ref, lse_ref, delta_ref, do_ref, q_ref, *refs):
    kv_refs, refs = refs[:parts], refs[parts:]
    dq_ref, own_ref = refs[:2]
    other_refs = refs[2 : 1 + parts]
    k_nat, v_nat, pair, dq_acc, dkv = refs[1 + parts :]
    tokens = kv_refs[0].shape[-1]
    wide = GROUPS * tokens
    info = (info_ref[0], info_ref[1])
    for slot in range(rows * parts):
        k_nat[slot] = kv_refs[slot // rows][slot % rows, 0, :HEAD, :].T
        v_nat[slot] = kv_refs[slot // rows][slot % rows, 0, HEAD:, :].T
    dkv[...] = jnp.zeros_like(dkv)
    blank = jnp.zeros((wide, HEAD), BF16)

    for row in range(rows):
        mine, low, full = info_ref[2 + 3 * row], info_ref[3 + 3 * row], info_ref[4 + 3 * row]
        dq_acc[...] = jnp.zeros_like(dq_acc)
        start, place = spans_of(start_ref, row, mine)
        pair[:wide, :] = jnp.concatenate([q_ref[row, 0].T, blank], axis=1)
        pair[wide:, :] = jnp.concatenate([blank, do_ref[row, 0].T], axis=1)

        def step(block, masked):
            slot = slot_of(block, info, parts, rows)
            scores = mdot(k_nat[slot], q_ref[row, 0])
            back = mdot(v_nat[slot], do_ref[row, 0])
            weights = jnp.exp(scores - lse_ref[row, 0])
            if masked:
                allowed = visible(block, start, place, (tokens, wide))
                weights = jnp.where(allowed, weights, 0.0)
            slope = (weights * (back - delta_ref[row, 0])).astype(BF16)
            both = jnp.concatenate([slope, weights.astype(BF16)], axis=1)
            dkv[slot] += mdot(both, pair[...])
            return slope, slot

        def masked_step(block, carry):
            slope, slot = step(block, True)
            dq_acc[...] += mdot(k_nat[slot].T, slope)
            return carry

        def two_steps(index, carry):
            block = middle + 2 * index
            one, slot_one = step(block, False)
            two, slot_two = step(block + 1, False)
            turned = jnp.concatenate([k_nat[slot_one].T, k_nat[slot_two].T], axis=1)
            dq_acc[...] += mdot(turned, jnp.concatenate([one, two], axis=0))
            return carry

        middle = jnp.minimum(full, mine)
        count = mine - middle
        lax.fori_loop(low, middle, masked_step, 0)
        lax.fori_loop(0, count // 2, two_steps, 0)

        @pl.when(count % 2 == 1)
        def _():
            slope, slot = step(mine - 1, False)
            dq_acc[...] += mdot(k_nat[slot].T, slope)

        masked_step(mine, 0)
        cos, sin = cos_ref[row], sin_ref[row]
        for group in range(GROUPS):
            lanes = slice(group * tokens, (group + 1) * tokens)
            a = dq_acc[:HALF, lanes] * 0.125
            b = dq_acc[HALF:, lanes] * 0.125
            dq_ref[row, group * HEAD : group * HEAD + HALF, :] = (a * cos + b * sin).astype(BF16)
            dq_ref[row, group * HEAD + HALF : (group + 1) * HEAD, :] = (b * cos - a * sin).astype(BF16)
    own_ref[...] = dkv[:rows]
    for i, other_ref in enumerate(other_refs):
        other_ref[...] = dkv[(i + 1) * rows : (i + 2) * rows].astype(BF16)


def attention_calls(rows, parts, tokens):
    wide = GROUPS * tokens
    slots = rows * parts
    pair_work = rows * (slots + 1) / 2 * tokens * tokens * HEADS * HEAD
    attend = call(
        functools.partial(attend_body, parts, rows),
        [((rows, KV_HEADS, HEAD, wide), BF16), ((rows, KV_HEADS, 1, wide), F32)],
        [SM] + [VM] * (2 + parts),
        scratch=[
            pltpu.VMEM((slots, KV_HEADS, tokens, HEAD), BF16),
            pltpu.VMEM((slots, KV_HEADS, HEAD + SUM_ROWS, tokens), BF16),
            pltpu.VMEM((KV_HEADS, HEAD + SUM_ROWS, wide), F32),
        ],
        cost=estimate(4 * 4 * pair_work, 4e6, pair_work / HEAD),
    )

    def attend_back(head, *args):
        one_head = lambda *shape: pl.BlockSpec(
            (rows, 1, *shape), lambda i: (0, head) + (0,) * len(shape)
        )
        return call(
            functools.partial(attend_back_body, parts, rows),
            [
                ((rows, GROUPS * HEAD, tokens), BF16),
                ((rows, tokens, 2 * HEAD), F32),
                *[((rows, tokens, 2 * HEAD), BF16)] * (parts - 1),
            ],
            [
                SM, whole(rows, tokens), whole(rows, HALF, tokens),
                whole(rows, HALF, tokens), one_head(1, wide), one_head(1, wide),
                one_head(HEAD, wide), one_head(HEAD, wide), *[one_head(2 * HEAD, tokens)] * parts,
            ],
            [whole(rows, GROUPS * HEAD, tokens)] + [whole(rows, tokens, 2 * HEAD)] * parts,
            scratch=[
                pltpu.VMEM((slots, tokens, HEAD), BF16),
                pltpu.VMEM((slots, tokens, HEAD), BF16),
                pltpu.VMEM((2 * wide, 2 * HEAD), BF16),
                pltpu.VMEM((HEAD, wide), F32),
                pltpu.VMEM((slots, tokens, 2 * HEAD), F32),
            ],
            grid=(1,),
            cost=estimate(10 * 4 * pair_work / KV_HEADS, 3e6, pair_work / HEAD / KV_HEADS),
        )(*args)

    return attend, attend_back


def column(ref):
    return jnp.broadcast_to(ref[...], (8, ref.shape[1])).T[:, :1]


def keep_and_send(core, first, second):
    return jnp.where(core == 0, first, second), jnp.where(core == 0, second, first)


def feed_body(rows, core_ref, o_ref, gain_ref, wo_ref, wg_ref, wu_ref, wd_ref, *refs):
    x_refs, g_refs, refs = refs[:rows], refs[rows : 2 * rows], refs[2 * rows :]
    out_refs, refs = refs[:rows], refs[rows:]
    keep_ref, send_ref, grad, middle, back_acc, out_acc, normed, hid, dgate, dup = refs
    tokens = x_refs[0].shape[1]
    step = pl.program_id(0)
    spans = [slice(row * tokens, (row + 1) * tokens) for row in range(rows)]

    @pl.when(step == 0)
    def _():
        turned = wo_ref[...].T
        gain = column(gain_ref)
        for row, lanes in enumerate(spans):
            grad[:, lanes] = g_refs[row][...]
            mixed = jnp.concatenate(
                [
                    o_ref[row, head // GROUPS, :, (head % GROUPS) * tokens : (head % GROUPS + 1) * tokens]
                    for head in range(HEADS)
                ],
                axis=0,
            )
            total = x_refs[row][...].astype(F32) + mdot(turned, mixed)
            middle[:, lanes] = total
            out_acc[:, lanes] = total
            normed[:, lanes] = (total * rms_factor(total) * gain).astype(BF16)
        back_acc[...] = jnp.zeros_like(back_acc)

    wg_t, wu_t, wd_t = wg_ref[...].T, wu_ref[...].T, wd_ref[...].T
    for lanes in spans:
        source = normed[:, lanes]
        gate, up = mdot(wg_t, source), mdot(wu_t, source)
        dhidden = mdot(wd_t, grad[:, lanes])
        sig = jax.nn.sigmoid(gate)
        silu = gate * sig
        hid[:, lanes] = (silu * up).astype(BF16)
        dgate[:, lanes] = (dhidden * up * (sig + silu * (1.0 - sig))).astype(BF16)
        dup[:, lanes] = (dhidden * silu).astype(BF16)
    for lanes in spans:
        out_acc[:, lanes] += mdot(wd_ref[...], hid[:, lanes])
        back_acc[:, lanes] += mdot(wg_ref[...], dgate[:, lanes]) + mdot(wu_ref[...], dup[:, lanes])
    half = keep_ref.shape[0] // 3
    for i, (left, right) in enumerate(((normed, dgate), (normed, dup), (grad, hid))):
        value = rdot(left[...], right[...]).astype(BF16)
        span = slice(i * half, (i + 1) * half)
        keep_ref[span], send_ref[span] = keep_and_send(core_ref[0], value[:half], value[half:])

    @pl.when(step == pl.num_programs(0) - 1)
    def _():
        for out_ref, lanes in zip(out_refs, spans):
            out_ref[...] = out_acc[:, lanes].astype(BF16)


def feed_call(rows, tokens, width, hidden, chunks):
    count, wide, chunk = rows * tokens, GROUPS * tokens, hidden // chunks
    columns = pl.BlockSpec((width, chunk), lambda i: (0, i))
    half = pl.BlockSpec((3 * width // 2, chunk), lambda i: (0, i))
    return call(
        functools.partial(feed_body, rows),
        [
            *[((width, tokens), BF16)] * rows, *[((3 * width // 2, hidden), BF16)] * 2,
            ((width, count), BF16), *[((width, count), F32)] * 2,
        ],
        [
            SM, whole(rows, KV_HEADS, HEAD, wide), whole(1, width), whole(width, width),
            columns, columns, columns, *[whole(width, tokens)] * (2 * rows),
        ],
        [*[whole(width, tokens)] * rows, half, half, *[whole(width, count)] * 3],
        scratch=[
            pltpu.VMEM((width, count), F32), pltpu.VMEM((width, count), BF16), *[pltpu.VMEM((chunk, count), BF16)] * 3,
        ],
        grid=(chunks,),
        cost=estimate(2 * count * 9 * width * hidden, 3e7, count * hidden),
    )


def turn_body(rows, o_ref, grad, middle, back_acc, gain_ref, wo_ref, *refs):
    og_ref, dmid_ref, do_ref, delta_ref, two_ref, branches = refs
    tokens = dmid_ref.shape[-1]
    step = pl.program_id(0)
    gain = column(gain_ref)
    source = middle[...]
    dnormed = back_acc[...]
    scale = rms_factor(source)
    two = jnp.sum(dnormed * source * scale, axis=1, keepdims=True)
    dmiddle = grad[...].astype(F32) + norm_back(source, scale, gain, dnormed)
    dmid_ref[0] = dmiddle
    branch = dmiddle.astype(BF16)
    dattended = mdot(wo_ref[...], branch).astype(BF16)
    mixed = jnp.concatenate(
        [
            o_ref[0, head // GROUPS, :, (head % GROUPS) * tokens : (head % GROUPS + 1) * tokens]
            for head in range(HEADS)
        ],
        axis=0,
    )
    product = dattended.astype(F32) * mixed.astype(F32)
    for head in range(HEADS):
        kv, lane = head // GROUPS, (head % GROUPS) * tokens
        span = slice(head * HEAD, (head + 1) * HEAD)
        do_ref[0, kv, :, lane : lane + tokens] = dattended[span]
        delta_ref[0, kv, :, lane : lane + tokens] = jnp.sum(product[span], axis=0, keepdims=True)
    og = rdot(mixed, branch)

    @pl.when(step == 0)
    def _():
        two_ref[...] = two
        branches[...] = og

    @pl.when(step > 0)
    def _():
        two_ref[...] += two
        branches[...] += og

    @pl.when(step == rows - 1)
    def _():
        og_ref[...] = branches[...].astype(BF16)


def turn_call(rows, tokens, width):
    count, wide = rows * tokens, GROUPS * tokens
    block = pl.BlockSpec((width, tokens), lambda i: (0, i))
    part = lambda *shape: pl.BlockSpec((1, *shape), lambda i: (i,) + (0,) * len(shape))
    return call(
        functools.partial(turn_body, rows),
        [
            ((width, width), BF16),
            ((rows, width, tokens), F32),
            ((rows, KV_HEADS, HEAD, wide), BF16),
            ((rows, KV_HEADS, 1, wide), F32),
            ((width, 1), F32),
        ],
        [part(KV_HEADS, HEAD, wide), *[block] * 3, whole(1, width), whole(width, width)],
        [
            whole(width, width), part(width, tokens),
            part(KV_HEADS, HEAD, wide), part(KV_HEADS, 1, wide), whole(width, 1),
        ],
        scratch=[pltpu.VMEM((width, width), F32)],
        grid=(rows,),
        cost=estimate(4 * count * width * width, 1.2e7),
    )


def last_body(rows, parts, core_ref, normed_ref, cos_ref, sin_ref, gain_ref, wq_ref, wk_ref, wv_ref, og_ref, two_ref, *refs):
    dq_refs, refs = refs[:KV_HEADS], refs[KV_HEADS:]
    own_refs, refs = refs[:KV_HEADS], refs[KV_HEADS:]
    other_refs, refs = refs[: KV_HEADS * (parts - 1)], refs[KV_HEADS * (parts - 1) :]
    keep_ref, send_ref, dkv_ref, query_acc, pair_acc = refs
    step = pl.program_id(0)
    width = normed_ref.shape[1]

    @pl.when(step == 0)
    def _():
        query_acc[...] = jnp.zeros_like(query_acc)
        pair_acc[...] = jnp.zeros_like(pair_acc)

    dq = jnp.concatenate([ref[0] for ref in dq_refs], axis=0)
    cos, sin = cos_ref[0], sin_ref[0]
    keys, values = [], []
    for head in range(KV_HEADS):
        turned = own_refs[head][0]
        for i in range(parts - 1):
            turned = turned + other_refs[head * (parts - 1) + i][0].astype(F32)
        turned = turned.T
        a, b = turned[:HALF], turned[HALF:HEAD]
        keys += [a * cos + b * sin, b * cos - a * sin]
        values.append(turned[HEAD:])
    dkv = jnp.concatenate(keys + values, axis=0).astype(BF16)
    dkv_ref[0] = dkv
    normed = normed_ref[0]
    query_acc[...] += rdot(normed, dq)
    pair_acc[...] += rdot(dkv, normed)

    @pl.when(step == pl.num_programs(0) - 1)
    def _():
        one = jnp.sum(wq_ref[...].astype(F32) * query_acc[...], axis=1, keepdims=True)
        weights = jnp.concatenate([wk_ref[...], wv_ref[...]], axis=0).astype(F32)
        more = jnp.sum(weights * pair_acc[...], axis=0, keepdims=True)
        one = (one + jnp.broadcast_to(more, (8, width)).T[:, :1]) / column(gain_ref)
        query, pair = query_acc[...].astype(BF16), pair_acc[...].astype(BF16)
        half = keep_ref.shape[0]
        cut = half - width
        spare = keep_ref.shape[1] - width
        lane = lax.broadcasted_iota(jnp.int32, (width, spare), 1)
        gains = jnp.where(lane == 0, one, jnp.where(lane == 1, two_ref[...], 0.0))
        blank = jnp.zeros((half, spare), BF16)
        low = jnp.concatenate([og_ref[...], query[:cut]], axis=0)
        low = jnp.concatenate(
            [low, jnp.concatenate([gains.astype(BF16), blank[:cut]], axis=0)], axis=1
        )
        high = jnp.concatenate([query[cut:], pair], axis=0)
        high = jnp.concatenate([high, blank], axis=1)
        keep_ref[...], send_ref[...] = keep_and_send(core_ref[0], low, high)


def last_call(rows, parts, tokens, width, lanes):
    kv_width = KV_HEADS * HEAD
    part = lambda *shape: pl.BlockSpec((1, *shape), lambda i: (i,) + (0,) * len(shape))
    return call(
        functools.partial(last_body, rows, parts),
        [*[((width + kv_width, lanes), BF16)] * 2, ((rows, 2 * kv_width, tokens), BF16)],
        [
            SM, part(width, tokens), part(HALF, tokens), part(HALF, tokens), whole(1, width),
            whole(width, width), whole(kv_width, width), whole(kv_width, width),
            whole(width, width), whole(width, 1),
            *[part(kv_width, tokens)] * KV_HEADS, *[part(tokens, 2 * HEAD)] * (KV_HEADS * parts),
        ],
        [*[whole(width + kv_width, lanes)] * 2, part(2 * kv_width, tokens)],
        scratch=[pltpu.VMEM((width, width), F32), pltpu.VMEM((2 * kv_width, width), F32)],
        grid=(rows,),
        cost=estimate(2 * rows * tokens * 5.6e5, 1e7),
    )


def input_body(rows, x_ref, dmid_ref, gain_ref, wq_ref, wkv_ref, dkv_ref, *refs):
    dq_refs, ig_refs = refs[:KV_HEADS], refs[KV_HEADS:]
    step = pl.program_id(0)
    dq = jnp.concatenate([ref[0] for ref in dq_refs], axis=0)
    dnormed = mdot(wq_ref[...], dq) + mdot(wkv_ref[...], dkv_ref[0])
    x = x_ref[0].astype(F32)
    ig = (dmid_ref[0] + norm_back(x, rms_factor(x), column(gain_ref), dnormed)).astype(BF16)
    for row in range(rows):

        @pl.when(step == row)
        def _():
            ig_refs[row][...] = ig


def input_call(rows, tokens, width):
    kv_width = KV_HEADS * HEAD
    part = lambda *shape: pl.BlockSpec((1, *shape), lambda i: (i,) + (0,) * len(shape))
    return call(
        functools.partial(input_body, rows),
        [((width, tokens), BF16)] * rows,
        [
            part(width, tokens), part(width, tokens), whole(1, width), whole(width, width),
            whole(width, 2 * kv_width), part(2 * kv_width, tokens),
            *[part(kv_width, tokens)] * KV_HEADS,
        ],
        [whole(width, tokens)] * rows,
        grid=(rows,),
        cost=estimate(2 * rows * tokens * 5.6e5, 1e7),
    )


def bit_length(size):
    return [1 << i for i in range(size.bit_length() - 1)]


def swap(value, axis, bit):
    size = lax.axis_size(axis)
    return lax.ppermute(value, axis, [(i, i ^ bit) for i in range(size)])


def pick(value, index):
    return lax.dynamic_index_in_dim(value, index, 0, keepdims=False)


def after(value, *others):
    return lax.optimization_barrier((value, *others))[0]


def join(*trees):
    return lax.optimization_barrier(trees)


def place_body(count, copies, mine_ref, *refs):
    out_ref = refs[count]
    for k in range(count):
        value = refs[k][...].astype(out_ref.dtype)
        for i in range(copies):
            out_ref[i, mine_ref[0] ^ k] = value


def placed(pieces, mine, dtype=BF16, copies=1):
    count = len(pieces)
    return call(
        functools.partial(place_body, count, copies),
        [((copies, count, *pieces[0].shape), dtype)],
        [SM] + [VM] * count,
        cost=estimate(0, 2 * (1 + copies) * count * pieces[0].size),
    )(mine.reshape(1), *pieces)[0]


def unpack_body(core_ref, piece_ref, *refs):
    out_refs = refs[-3:]
    outer, inner = piece_ref.shape[:2]
    half = out_refs[0].shape[0]
    value = jnp.concatenate(
        [jnp.concatenate([piece_ref[i, j] for j in range(inner)], axis=1) for i in range(outer)],
        axis=0,
    ).astype(F32)
    for i, out_ref in enumerate(out_refs):
        out_ref[...] = value[i * half : (i + 1) * half]


def unpack(core, piece, width, hidden, sums=()):
    outer, inner, rows, lanes = piece.shape
    each = 1 if lanes % 128 == 0 else 2
    block = pl.BlockSpec((width // 2, each * lanes), lambda i, core_ref: (core_ref[0], i))
    return pl.pallas_call(
        unpack_body,
        out_shape=[jax.ShapeDtypeStruct((width, hidden), F32)] * 3,
        grid_spec=pltpu.PrefetchScalarGridSpec(
            num_scalar_prefetch=1,
            grid=(inner // each,),
            in_specs=[
                pl.BlockSpec((outer, each, rows, lanes), lambda i, core_ref: (0, i, 0, 0)),
                *[pl.BlockSpec(memory_space=pl.ANY)] * len(sums),
            ],
            out_specs=[block] * 3,
        ),
        input_output_aliases={2 + i: i for i in range(len(sums))},
        compiler_params=pltpu.CompilerParams(vmem_limit_bytes=VMEM_LIMIT),
        cost_estimate=estimate(0, 9 * width * hidden),
    )(core, piece, *sums)


def tail_body(core_ref, mine_ref, other_ref, o_ref, q_ref, k_ref, v_ref, gain_ref):
    width, kv = o_ref.shape[1], k_ref.shape[0]
    even = core_ref[0] == 0
    low = jnp.where(even, mine_ref[...], other_ref[...]).astype(F32)
    high = jnp.where(even, other_ref[...], mine_ref[...]).astype(F32)
    cut = low.shape[0] - width
    o_ref[...] = low[:width, :width]
    gain_ref[...] = low[:width, width:].T
    q_ref[:cut] = low[width:, :width]
    q_ref[cut:] = high[: width - cut, :width]
    k_ref[...] = high[width - cut : width - cut + kv, :width]
    v_ref[...] = high[width - cut + kv :, :width]


class Axis:
    def __init__(self, name, bit):
        self.name, self.bit = name, bit
        self.size = lax.axis_size(name) // bit
        self.mine = lax.axis_index(name) // bit
        self.groups = None
        if bit > 1:
            self.groups = [[c + bit * i for i in range(self.size)] for c in range(bit)]

    def trade(self, value):
        return lax.all_to_all(value, self.name, 0, 0, tiled=True, axis_index_groups=self.groups)

    def spread(self, value):
        return self.trade(jnp.broadcast_to(value, (self.size, *value.shape)))

    def send_parts(self, value):
        return [pick(value, self.mine)] + [
            swap(pick(value, self.mine ^ k), self.name, k * self.bit)
            for k in range(1, self.size)
        ]

    def send_all(self, value):
        return [value] + [swap(value, self.name, k * self.bit) for k in range(1, self.size)]


def total(pieces):
    result = pieces[0].astype(F32)
    for piece in pieces[1:]:
        result = result + piece.astype(F32)
    return result.astype(BF16)


def folded(value):
    return jnp.sum(value.astype(F32), axis=0).astype(BF16)


def split_columns(value, size):
    return jnp.swapaxes(value.reshape(value.shape[0], size, -1), 0, 1)


def shards(
    inputs, doc_lengths, gain_one, gain_two, w_query, w_key, w_value, w_out, w_gate, w_up, w_down, cotangent
):
    rows, tokens, width = inputs.shape
    hidden = w_gate.shape[1]
    seq = lax.axis_size("seq")
    batch = lax.axis_size("batch")
    parts = seq // rows
    me = lax.axis_index("seq")
    group, part = me // parts, me % parts
    wide = GROUPS * tokens
    kv_width = KV_HEADS * HEAD

    def dealt(block):
        g, place = block // parts, block % parts
        return g, place if g % 2 == 0 else parts - 1 - place

    def route(step):
        pairs = []
        for block in range(seq):
            g, p = dealt(block)
            pairs.append((block, (g ^ step) * parts + p))
        return pairs

    def bring(value):
        return [lax.ppermute(pick(value, group ^ step), "seq", route(step)) for step in range(rows)]

    def back(pieces):
        return [
            lax.ppermute(piece, "seq", [(b, a) for a, b in route(step)])
            for step, piece in enumerate(pieces)
        ]

    def place_rows(pieces, dtype):
        return jnp.swapaxes(placed(pieces, group, dtype)[0], 1, 2)

    x_parts = bring(jnp.swapaxes(inputs, 1, 2))

    groups_here = group ^ jnp.arange(rows, dtype=jnp.int32)
    blocks = groups_here * parts + jnp.where(groups_here % 2 == 0, part, parts - 1 - part)
    lengths = pick(doc_lengths, group)
    order = jnp.arange(lengths.shape[0])
    ends = jnp.sum(jnp.where(order[None, :] <= order[:, None], lengths[None, :], 0), axis=1)
    places = blocks[:, None] * tokens + jnp.arange(tokens, dtype=jnp.int32)[None, :]
    starts = jnp.sum(jnp.where(ends <= places[..., None], lengths, 0), axis=-1)
    info = jnp.concatenate(
        [
            jnp.stack([group, part]),
            jnp.stack(
                [blocks, starts[:, 0] // tokens, (starts[:, -1] + tokens - 1) // tokens], axis=1
            ).reshape(-1),
        ]
    ).astype(jnp.int32)
    inverse = 1.0 / ROPE_BASE ** (jnp.arange(HALF, dtype=F32) * (2.0 / HEAD))
    angles = (places - starts).astype(F32)[:, None, :] * inverse[None, :, None]
    cos_t, sin_t = jnp.cos(angles), jnp.sin(angles)
    gain_a = gain_one.astype(F32)[None, :]
    gain_b = gain_two.astype(F32)[None, :]
    w_pair = jnp.concatenate([w_key, w_value], axis=1)
    core = (me % 2).reshape(1)
    ready = (info, starts, cos_t, sin_t, gain_a, gain_b, w_pair, w_query.T)
    cotangent = join(cotangent, x_parts[1])[0]
    x_parts, ready = join(x_parts, ready)
    info, starts, cos_t, sin_t, gain_a, gain_b, w_pair, w_query_t = ready
    g_parts = bring(jnp.swapaxes(cotangent, 1, 2))

    x_all, normed, kv = call(
        functools.partial(pair_body, rows),
        [*[((rows, width, tokens), BF16)] * 2, ((rows, KV_HEADS, 2 * HEAD, tokens), BF16)],
        [VM] * (5 + rows),
        cost=estimate(4 * rows * tokens * width * kv_width, 3e6),
    )(gain_a, w_key.T, w_value.T, cos_t, sin_t, *x_parts)

    def ring(i, value):
        pairs = [
            (r * parts + (p + i) % parts, r * parts + p) for r in range(rows) for p in range(parts)
        ]
        return lax.ppermute(value, "seq", pairs)

    kv_all = [kv] + [ring(i, kv) for i in range(1, parts)]
    q = call(
        functools.partial(query_body, rows),
        [((rows, KV_HEADS, HEAD, wide), BF16)],
        [VM] * 4,
        cost=estimate(2 * rows * tokens * width * width, 3e6),
    )(normed, w_query_t, cos_t, sin_t)[0]
    q, kv_all = join(q, kv_all)

    attend, attend_back = attention_calls(rows, parts, tokens)
    o, lse = attend(info, starts, q, *kv_all)
    o, g_parts = join(o, g_parts)

    plane, line = Axis("seq", 2), Axis("batch", 1)
    count = rows * tokens
    *out, keep, send, grad, middle, back_acc = feed_call(rows, tokens, width, hidden, 2)(
        core, o, gain_b, w_out, w_gate, w_up, w_down.T, *x_parts, *g_parts
    )
    send, back_acc = join(send, back_acc)
    got = swap(send, "seq", 1)
    og, dmiddle, do, delta, two = turn_call(rows, tokens, width)(
        o, grad, middle, back_acc, gain_b, w_out
    )
    got, do = join(got, do)
    part = total([keep, got]).reshape(plane.size, -1, hidden)
    part, do = join(part, do)
    trade = plane.trade(part)

    def back_call(head, do):
        return attend_back(head, info, starts, cos_t, sin_t, lse, delta, do, q, *kv_all)

    def deliver(others):
        got = []
        for i, other in enumerate(others, 1):
            pairs = [
                (r * parts + p, r * parts + (p + i) % parts)
                for r in range(rows)
                for p in range(parts)
            ]
            got.append(lax.ppermute(other, "seq", pairs))
        return got

    dq0, own0, *others0 = back_call(0, do)
    dq0, do = join(dq0, do)
    got0 = deliver(others0)
    dq1, own1, *others1 = back_call(1, do)
    trade, dq1, own1, others1, do, out = join(trade, dq1, own1, others1, do, out)
    part = split_columns(folded(trade), batch)
    part, others1, do, out = join(part, others1, do, out)
    got1 = deliver(others1)
    pieces = line.trade(part)
    out_back = back(out)
    dq2, own2, *others2 = back_call(2, do)
    pieces, dq2, own2, others2, out_back = join(pieces, dq2, own2, others2, out_back)
    output = place_rows(out_back, BF16)
    part = folded(pieces)
    part, dq2, others2 = join(part, dq2, others2)
    got2 = deliver(others2)
    pieces = line.send_all(part)
    lanes = -(-width // 128) * 128
    keep, send, dkv = last_call(rows, parts, tokens, width, lanes)(
        core, normed, cos_t, sin_t, gain_a, w_query, w_key.T, w_value.T, og, two,
        dq0, dq1, dq2, own0, own1, own2, *got0, *got1, *got2,
    )
    send, dkv, keep = join(send, dkv, keep)
    got = swap(send, "seq", 1)
    ig = input_call(rows, tokens, width)(
        x_all, dmiddle, gain_a, w_query, w_pair, dkv, dq0, dq1, dq2
    )
    got, keep, ig = join(got, keep, ig)
    tail = total([keep, got]).reshape(plane.size, -1, lanes)
    tail, ig = join(tail, ig)
    trade = plane.trade(tail)
    ig_back = back(ig)
    trade, pieces, output, ig_back = join(trade, pieces, output, ig_back)
    tail = folded(trade).reshape(batch, -1, lanes)
    part = placed(pieces, line.mine, copies=plane.size)
    tail, part = join(tail, part)
    tail_pieces = line.send_parts(tail)
    feed_all = plane.trade(part)
    tail_pieces = line.send_all(total(tail_pieces))
    tail = placed(tail_pieces, line.mine)[0].reshape(-1, lanes)
    tail_pieces = plane.send_all(tail)
    input_grad = place_rows(ig_back, F32)
    tail_pieces, input_grad, feed_all = join(tail_pieces, input_grad, feed_all)
    tail_all = placed(tail_pieces, plane.mine)[0].reshape(-1, lanes)
    tail_all, feed_all = join(tail_all, feed_all)
    tail_other = swap(tail_all, "seq", 1)
    feed_other = swap(feed_all, "seq", 1)
    sums = unpack(core, feed_all, width, hidden)
    sums, tail_other, feed_other = join(sums, tail_other, feed_other)
    w_gate_sum, w_up_sum, w_down_sum = unpack(1 - core, feed_other, width, hidden, sums)
    w_out_sum, w_query_sum, w_key_sum, w_value_sum, gains = call(
        tail_body,
        [
            *[((width, width), F32)] * 2,
            *[((kv_width, width), F32)] * 2,
            ((lanes - width, width), F32),
        ],
        [SM, VM, VM],
        cost=estimate(0, 6e6),
    )(core, tail_all, tail_other)
    return (
        output,
        input_grad,
        gains[0],
        gains[1],
        w_query_sum,
        w_key_sum.T,
        w_value_sum.T,
        w_out_sum,
        w_gate_sum,
        w_up_sum,
        w_down_sum.T,
    )


def solution(mesh):
    tokens_spec = P("batch", "seq", None)
    return jax.shard_map(
        shards,
        mesh=mesh,
        in_specs=(tokens_spec, P("batch", None), *([P()] * 9), tokens_spec),
        out_specs=(tokens_spec, tokens_spec, *([P()] * 9)),
        check_vma=False,
    )
```

```python
import functools
import math

import jax
import jax.numpy as jnp
from jax import lax
from jax.experimental import pallas as pl
from jax.experimental.pallas import tpu as pltpu
from jax.sharding import PartitionSpec as P

HEADS = 9
KV_HEADS = 3
HEAD = 64
GROUPS = HEADS // KV_HEADS
HALF = HEAD // 2
EPSILON = 1e-05
ROPE_BASE = 10000.0
FAR_NEGATIVE = -1e30
SUM_ROWS = 16

F32 = jnp.float32
BF16 = jnp.bfloat16
VMEM_LIMIT = 56 * 1024 * 1024


def rms_factor(values):
    return lax.rsqrt(jnp.mean(values * values, axis=0, keepdims=True) + EPSILON)


def norm_back(source, factor, gain_value, upstream):
    scaled = upstream * gain_value
    return factor * scaled - source * factor * factor * factor * jnp.mean(
        scaled * source, axis=0, keepdims=True
    )


def mdot(left, right):
    return jnp.dot(left, right, preferred_element_type=F32)


def tdot(left, right):
    return lax.dot_general(left, right, (((0,), (0,)), ((), ())), preferred_element_type=F32)


def rdot(left, right):
    return lax.dot_general(left, right, (((1,), (1,)), ((), ())), preferred_element_type=F32)


VM = pl.BlockSpec(memory_space=pltpu.VMEM)
SM = pl.BlockSpec(memory_space=pltpu.SMEM)


def call(body, outs, in_specs, out_specs=None, scratch=(), cost=None, **more):
    return pl.pallas_call(
        body,
        out_shape=[jax.ShapeDtypeStruct(*o) for o in outs],
        in_specs=in_specs,
        out_specs=out_specs or [VM] * len(outs),
        scratch_shapes=list(scratch),
        compiler_params=pltpu.CompilerParams(vmem_limit_bytes=VMEM_LIMIT),
        cost_estimate=cost,
        **more,
    )


def whole(*shape):
    return pl.BlockSpec(shape, lambda *unused: (0,) * len(shape))


def estimate(flops, nbytes, trans=0):
    return pl.CostEstimate(
        flops=int(flops), bytes_accessed=int(nbytes), transcendentals=int(trans)
    )


def pair_body(rows, gain_ref, wk_ref, wv_ref, cos_ref, sin_ref, *refs):
    gain = column(gain_ref)
    weights = jnp.concatenate([wk_ref[...], wv_ref[...]], axis=0)
    x_refs, (x_all, normed_ref, kv_ref) = refs[:rows], refs[rows:]
    for row in range(rows):
        x_all[row] = x_refs[row][...]
        x = x_refs[row][...].astype(F32)
        normed = (x * rms_factor(x) * gain).astype(BF16)
        normed_ref[row] = normed
        turned = mdot(weights, normed)
        cos, sin = cos_ref[row], sin_ref[row]
        for head in range(KV_HEADS):
            at = head * HEAD
            a, b = turned[at : at + HALF], turned[at + HALF : at + HEAD]
            kv_ref[row, head, :HALF, :] = (a * cos - b * sin).astype(BF16)
            kv_ref[row, head, HALF:HEAD, :] = (b * cos + a * sin).astype(BF16)
            at += KV_HEADS * HEAD
            kv_ref[row, head, HEAD:, :] = turned[at : at + HEAD].astype(BF16)


def query_body(rows, normed_ref, w_ref, cos_ref, sin_ref, q_ref):
    tokens = normed_ref.shape[-1]
    for row in range(rows):
        turned = mdot(w_ref[...], normed_ref[row])
        cos, sin = cos_ref[row] * 0.125, sin_ref[row] * 0.125
        for head in range(HEADS):
            a = turned[head * HEAD : head * HEAD + HALF]
            b = turned[head * HEAD + HALF : (head + 1) * HEAD]
            kv, lane = head // GROUPS, (head % GROUPS) * tokens
            q_ref[row, kv, :HALF, lane : lane + tokens] = (a * cos - b * sin).astype(BF16)
            q_ref[row, kv, HALF:, lane : lane + tokens] = (b * cos + a * sin).astype(BF16)


def owner(block, parts):
    group, place = block // parts, block % parts
    return jnp.where(group % 2 == 0, place, parts - 1 - place)


def slot_of(block, info, parts, rows):
    relative = (owner(block, parts) - info[1] + parts) % parts
    return relative * rows + ((block // parts) ^ info[0])


def spans_of(starts_ref, row, mine):
    start = jnp.concatenate([starts_ref[pl.ds(row, 1), :]] * GROUPS, axis=1)
    tokens = starts_ref.shape[1]
    lane = lax.broadcasted_iota(jnp.int32, start.shape, 1)
    return start, mine * tokens + lane % tokens


def visible(block, start, place, shape):
    key_place = block * shape[0] + lax.broadcasted_iota(jnp.int32, shape, 0)
    return (key_place >= start) & (key_place <= place)


def attend_body(parts, rows, info_ref, start_ref, q_ref, *refs):
    kv_refs, refs = refs[:parts], refs[parts:]
    o_ref, lse_ref, k_nat, v_aug, acc = refs
    tokens = kv_refs[0].shape[-1]
    info = (info_ref[0], info_ref[1])
    ones = (lax.broadcasted_iota(jnp.int32, (SUM_ROWS, tokens), 0) == 0).astype(BF16)
    for slot in range(rows * parts):
        kv_ref = kv_refs[slot // rows].at[slot % rows]
        for head in range(KV_HEADS):
            k_nat[slot, head] = kv_ref[head, :HEAD, :].T
            v_aug[slot, head, :HEAD, :] = kv_ref[head, HEAD:, :]
            v_aug[slot, head, HEAD:, :] = ones

    def per_row(row, carry):
        mine, low, full = info_ref[2 + 3 * row], info_ref[3 + 3 * row], info_ref[4 + 3 * row]
        acc[...] = jnp.zeros_like(acc)
        start, place = spans_of(start_ref, row, mine)

        def step(block, tops, masked):
            slot = slot_of(block, info, parts, rows)
            allowed = visible(block, start, place, (tokens, start.shape[-1])) if masked else None
            result = []
            for head in range(KV_HEADS):
                scores = mdot(k_nat[slot, head], q_ref[row, head])
                if masked:
                    scores = jnp.where(allowed, scores, FAR_NEGATIVE)
                top = jnp.maximum(tops[head], jnp.max(scores, axis=0, keepdims=True))
                weights = jnp.exp(scores - top).astype(BF16)
                acc[head] = acc[head] * jnp.exp(tops[head] - top) + mdot(v_aug[slot, head], weights)
                result.append(top)
            return tuple(result)

        tops = tuple(
            jnp.full((1, start.shape[-1]), FAR_NEGATIVE, F32) for unused in range(KV_HEADS)
        )
        middle = jnp.minimum(full, mine)
        tops = lax.fori_loop(low, middle, lambda b, s: step(b, s, True), tops)
        tops = lax.fori_loop(middle, mine, lambda b, s: step(b, s, False), tops)
        tops = step(mine, tops, True)
        for head in range(KV_HEADS):
            mass = acc[head, HEAD : HEAD + 1, :]
            o_ref[row, head] = (acc[head, :HEAD, :] / mass).astype(BF16)
            lse_ref[row, head] = tops[head] + jnp.log(mass)
        return carry

    lax.fori_loop(0, rows, per_row, 0)


def attend_back_body(parts, rows, info_ref, start_ref, cos_ref, sin_ref, lse_ref, delta_ref, do_ref, q_ref, *refs):
    kv_refs, refs = refs[:parts], refs[parts:]
    dq_ref, own_ref = refs[:2]
    other_refs = refs[2 : 1 + parts]
    k_nat, v_nat, pair, dq_acc, dkv = refs[1 + parts :]
    tokens = kv_refs[0].shape[-1]
    wide = GROUPS * tokens
    info = (info_ref[0], info_ref[1])
    for slot in range(rows * parts):
        k_nat[slot] = kv_refs[slot // rows][slot % rows, 0, :HEAD, :].T
        v_nat[slot] = kv_refs[slot // rows][slot % rows, 0, HEAD:, :].T
    dkv[...] = jnp.zeros_like(dkv)
    blank = jnp.zeros((wide, HEAD), BF16)

    def per_row(row, carry):
        mine, low, full = info_ref[2 + 3 * row], info_ref[3 + 3 * row], info_ref[4 + 3 * row]
        dq_acc[...] = jnp.zeros_like(dq_acc)
        start, place = spans_of(start_ref, row, mine)
        pair[:wide, :] = jnp.concatenate([q_ref[row, 0].T, blank], axis=1)
        pair[wide:, :] = jnp.concatenate([blank, do_ref[row, 0].T], axis=1)

        def step(block, masked):
            slot = slot_of(block, info, parts, rows)
            scores = mdot(k_nat[slot], q_ref[row, 0])
            back = mdot(v_nat[slot], do_ref[row, 0])
            weights = jnp.exp(scores - lse_ref[row, 0])
            if masked:
                allowed = visible(block, start, place, (tokens, wide))
                weights = jnp.where(allowed, weights, 0.0)
            slope = (weights * (back - delta_ref[row, 0])).astype(BF16)
            both = jnp.concatenate([slope, weights.astype(BF16)], axis=1)
            dkv[slot] += mdot(both, pair[...])
            return slope, slot

        def masked_step(block, carry):
            slope, slot = step(block, True)
            dq_acc[...] += mdot(k_nat[slot].T, slope)
            return carry

        def two_steps(index, carry):
            block = middle + 2 * index
            one, slot_one = step(block, False)
            two, slot_two = step(block + 1, False)
            turned = jnp.concatenate([k_nat[slot_one].T, k_nat[slot_two].T], axis=1)
            dq_acc[...] += mdot(turned, jnp.concatenate([one, two], axis=0))
            return carry

        middle = jnp.minimum(full, mine)
        count = mine - middle
        lax.fori_loop(low, middle, masked_step, 0)
        lax.fori_loop(0, count // 2, two_steps, 0)

        @pl.when(count % 2 == 1)
        def _():
            slope, slot = step(mine - 1, False)
            dq_acc[...] += mdot(k_nat[slot].T, slope)

        masked_step(mine, 0)
        cos, sin = cos_ref[row], sin_ref[row]
        for group in range(GROUPS):
            lanes = slice(group * tokens, (group + 1) * tokens)
            a = dq_acc[:HALF, lanes] * 0.125
            b = dq_acc[HALF:, lanes] * 0.125
            dq_ref[row, group * HEAD : group * HEAD + HALF, :] = (a * cos + b * sin).astype(BF16)
            dq_ref[row, group * HEAD + HALF : (group + 1) * HEAD, :] = (b * cos - a * sin).astype(BF16)
        return carry

    lax.fori_loop(0, rows, per_row, 0)
    own_ref[...] = dkv[:rows]
    for i, other_ref in enumerate(other_refs):
        other_ref[...] = dkv[(i + 1) * rows : (i + 2) * rows].astype(BF16)


def attention_calls(rows, parts, tokens):
    wide = GROUPS * tokens
    slots = rows * parts
    pair_work = rows * (slots + 1) / 2 * tokens * tokens * HEADS * HEAD
    attend = call(
        functools.partial(attend_body, parts, rows),
        [((rows, KV_HEADS, HEAD, wide), BF16), ((rows, KV_HEADS, 1, wide), F32)],
        [SM] + [VM] * (2 + parts),
        scratch=[
            pltpu.VMEM((slots, KV_HEADS, tokens, HEAD), BF16),
            pltpu.VMEM((slots, KV_HEADS, HEAD + SUM_ROWS, tokens), BF16),
            pltpu.VMEM((KV_HEADS, HEAD + SUM_ROWS, wide), F32),
        ],
        cost=estimate(4 * 4 * pair_work, 4e6, pair_work / HEAD),
    )

    def attend_back(head, *args):
        one_head = lambda *shape: pl.BlockSpec(
            (rows, 1, *shape), lambda i: (0, head) + (0,) * len(shape)
        )
        return call(
            functools.partial(attend_back_body, parts, rows),
            [
                ((rows, GROUPS * HEAD, tokens), BF16),
                ((rows, tokens, 2 * HEAD), F32),
                *[((rows, tokens, 2 * HEAD), BF16)] * (parts - 1),
            ],
            [
                SM, whole(rows, tokens), whole(rows, HALF, tokens),
                whole(rows, HALF, tokens), one_head(1, wide), one_head(1, wide),
                one_head(HEAD, wide), one_head(HEAD, wide), *[one_head(2 * HEAD, tokens)] * parts,
            ],
            [whole(rows, GROUPS * HEAD, tokens)] + [whole(rows, tokens, 2 * HEAD)] * parts,
            scratch=[
                pltpu.VMEM((slots, tokens, HEAD), BF16),
                pltpu.VMEM((slots, tokens, HEAD), BF16),
                pltpu.VMEM((2 * wide, 2 * HEAD), BF16),
                pltpu.VMEM((HEAD, wide), F32),
                pltpu.VMEM((slots, tokens, 2 * HEAD), F32),
            ],
            grid=(1,),
            cost=estimate(10 * 4 * pair_work / KV_HEADS, 3e6, pair_work / HEAD / KV_HEADS),
        )(*args)

    return attend, attend_back


def column(ref):
    return jnp.broadcast_to(ref[...], (8, ref.shape[1])).T[:, :1]


def keep_and_send(core, first, second):
    return jnp.where(core == 0, first, second), jnp.where(core == 0, second, first)


def feed_body(rows, core_ref, o_ref, gain_ref, wo_ref, wg_ref, wu_ref, wd_ref, *refs):
    x_refs, g_refs, refs = refs[:rows], refs[rows : 2 * rows], refs[2 * rows :]
    out_refs, refs = refs[:rows], refs[rows:]
    keep_ref, send_ref, grad, middle, back_acc, out_acc, normed, hid, dgate, dup = refs
    tokens = x_refs[0].shape[1]
    step = pl.program_id(0)
    spans = [slice(row * tokens, (row + 1) * tokens) for row in range(rows)]

    @pl.when(step == 0)
    def _():
        turned = wo_ref[...].T
        gain = column(gain_ref)
        for row, lanes in enumerate(spans):
            grad[:, lanes] = g_refs[row][...]
            mixed = jnp.concatenate(
                [
                    o_ref[row, head // GROUPS, :, (head % GROUPS) * tokens : (head % GROUPS + 1) * tokens]
                    for head in range(HEADS)
                ],
                axis=0,
            )
            total = x_refs[row][...].astype(F32) + mdot(turned, mixed)
            middle[:, lanes] = total
            out_acc[:, lanes] = total
            normed[:, lanes] = (total * rms_factor(total) * gain).astype(BF16)
        back_acc[...] = jnp.zeros_like(back_acc)

    wg_t, wu_t, wd_t = wg_ref[...].T, wu_ref[...].T, wd_ref[...].T
    for lanes in spans:
        source = normed[:, lanes]
        gate, up = mdot(wg_t, source), mdot(wu_t, source)
        dhidden = mdot(wd_t, grad[:, lanes])
        sig = jax.nn.sigmoid(gate)
        silu = gate * sig
        hid[:, lanes] = (silu * up).astype(BF16)
        dgate[:, lanes] = (dhidden * up * (sig + silu * (1.0 - sig))).astype(BF16)
        dup[:, lanes] = (dhidden * silu).astype(BF16)
    for lanes in spans:
        out_acc[:, lanes] += mdot(wd_ref[...], hid[:, lanes])
        back_acc[:, lanes] += mdot(wg_ref[...], dgate[:, lanes]) + mdot(wu_ref[...], dup[:, lanes])
    half = keep_ref.shape[0] // 3
    for i, (left, right) in enumerate(((normed, dgate), (normed, dup), (grad, hid))):
        value = rdot(left[...], right[...]).astype(BF16)
        span = slice(i * half, (i + 1) * half)
        keep_ref[span], send_ref[span] = keep_and_send(core_ref[0], value[:half], value[half:])

    @pl.when(step == pl.num_programs(0) - 1)
    def _():
        for out_ref, lanes in zip(out_refs, spans):
            out_ref[...] = out_acc[:, lanes].astype(BF16)


def feed_call(rows, tokens, width, hidden, chunks):
    count, wide, chunk = rows * tokens, GROUPS * tokens, hidden // chunks
    columns = pl.BlockSpec((width, chunk), lambda i: (0, i))
    half = pl.BlockSpec((3 * width // 2, chunk), lambda i: (0, i))
    return call(
        functools.partial(feed_body, rows),
        [
            *[((width, tokens), BF16)] * rows, *[((3 * width // 2, hidden), BF16)] * 2,
            ((width, count), BF16), *[((width, count), F32)] * 2,
        ],
        [
            SM, whole(rows, KV_HEADS, HEAD, wide), whole(1, width), whole(width, width),
            columns, columns, columns, *[whole(width, tokens)] * (2 * rows),
        ],
        [*[whole(width, tokens)] * rows, half, half, *[whole(width, count)] * 3],
        scratch=[
            pltpu.VMEM((width, count), F32), pltpu.VMEM((width, count), BF16), *[pltpu.VMEM((chunk, count), BF16)] * 3,
        ],
        grid=(chunks,),
        cost=estimate(2 * count * 9 * width * hidden, 3e7, count * hidden),
    )


def turn_body(rows, o_ref, grad, middle, back_acc, gain_ref, wo_ref, *refs):
    og_ref, dmid_ref, do_ref, delta_ref, two_ref, branches = refs
    tokens = dmid_ref.shape[-1]
    step = pl.program_id(0)
    gain = column(gain_ref)
    source = middle[...]
    dnormed = back_acc[...]
    scale = rms_factor(source)
    two = jnp.sum(dnormed * source * scale, axis=1, keepdims=True)
    dmiddle = grad[...].astype(F32) + norm_back(source, scale, gain, dnormed)
    dmid_ref[0] = dmiddle
    branch = dmiddle.astype(BF16)
    dattended = mdot(wo_ref[...], branch).astype(BF16)
    mixed = jnp.concatenate(
        [
            o_ref[0, head // GROUPS, :, (head % GROUPS) * tokens : (head % GROUPS + 1) * tokens]
            for head in range(HEADS)
        ],
        axis=0,
    )
    product = dattended.astype(F32) * mixed.astype(F32)
    for head in range(HEADS):
        kv, lane = head // GROUPS, (head % GROUPS) * tokens
        span = slice(head * HEAD, (head + 1) * HEAD)
        do_ref[0, kv, :, lane : lane + tokens] = dattended[span]
        delta_ref[0, kv, :, lane : lane + tokens] = jnp.sum(product[span], axis=0, keepdims=True)
    og = rdot(mixed, branch)

    @pl.when(step == 0)
    def _():
        two_ref[...] = two
        branches[...] = og

    @pl.when(step > 0)
    def _():
        two_ref[...] += two
        branches[...] += og

    @pl.when(step == rows - 1)
    def _():
        og_ref[...] = branches[...].astype(BF16)


def turn_call(rows, tokens, width):
    count, wide = rows * tokens, GROUPS * tokens
    block = pl.BlockSpec((width, tokens), lambda i: (0, i))
    part = lambda *shape: pl.BlockSpec((1, *shape), lambda i: (i,) + (0,) * len(shape))
    return call(
        functools.partial(turn_body, rows),
        [
            ((width, width), BF16),
            ((rows, width, tokens), F32),
            ((rows, KV_HEADS, HEAD, wide), BF16),
            ((rows, KV_HEADS, 1, wide), F32),
            ((width, 1), F32),
        ],
        [part(KV_HEADS, HEAD, wide), *[block] * 3, whole(1, width), whole(width, width)],
        [
            whole(width, width), part(width, tokens),
            part(KV_HEADS, HEAD, wide), part(KV_HEADS, 1, wide), whole(width, 1),
        ],
        scratch=[pltpu.VMEM((width, width), F32)],
        grid=(rows,),
        cost=estimate(4 * count * width * width, 1.2e7),
    )


def last_body(rows, parts, core_ref, normed_ref, cos_ref, sin_ref, gain_ref, wq_ref, wk_ref, wv_ref, og_ref, two_ref, *refs):
    dq_refs, refs = refs[:KV_HEADS], refs[KV_HEADS:]
    own_refs, refs = refs[:KV_HEADS], refs[KV_HEADS:]
    other_refs, refs = refs[: KV_HEADS * (parts - 1)], refs[KV_HEADS * (parts - 1) :]
    keep_ref, send_ref, dkv_ref, query_acc, pair_acc = refs
    step = pl.program_id(0)
    width = normed_ref.shape[1]

    @pl.when(step == 0)
    def _():
        query_acc[...] = jnp.zeros_like(query_acc)
        pair_acc[...] = jnp.zeros_like(pair_acc)

    dq = jnp.concatenate([ref[0] for ref in dq_refs], axis=0)
    cos, sin = cos_ref[0], sin_ref[0]
    keys, values = [], []
    for head in range(KV_HEADS):
        turned = own_refs[head][0]
        for i in range(parts - 1):
            turned = turned + other_refs[head * (parts - 1) + i][0].astype(F32)
        turned = turned.T
        a, b = turned[:HALF], turned[HALF:HEAD]
        keys += [a * cos + b * sin, b * cos - a * sin]
        values.append(turned[HEAD:])
    dkv = jnp.concatenate(keys + values, axis=0).astype(BF16)
    dkv_ref[0] = dkv
    normed = normed_ref[0]
    query_acc[...] += rdot(normed, dq)
    pair_acc[...] += rdot(dkv, normed)

    @pl.when(step == pl.num_programs(0) - 1)
    def _():
        one = jnp.sum(wq_ref[...].astype(F32) * query_acc[...], axis=1, keepdims=True)
        weights = jnp.concatenate([wk_ref[...], wv_ref[...]], axis=0).astype(F32)
        more = jnp.sum(weights * pair_acc[...], axis=0, keepdims=True)
        one = (one + jnp.broadcast_to(more, (8, width)).T[:, :1]) / column(gain_ref)
        query, pair = query_acc[...].astype(BF16), pair_acc[...].astype(BF16)
        half = keep_ref.shape[0]
        cut = half - width
        spare = keep_ref.shape[1] - width
        lane = lax.broadcasted_iota(jnp.int32, (width, spare), 1)
        gains = jnp.where(lane == 0, one, jnp.where(lane == 1, two_ref[...], 0.0))
        blank = jnp.zeros((half, spare), BF16)
        low = jnp.concatenate([og_ref[...], query[:cut]], axis=0)
        low = jnp.concatenate(
            [low, jnp.concatenate([gains.astype(BF16), blank[:cut]], axis=0)], axis=1
        )
        high = jnp.concatenate([query[cut:], pair], axis=0)
        high = jnp.concatenate([high, blank], axis=1)
        keep_ref[...], send_ref[...] = keep_and_send(core_ref[0], low, high)


def last_call(rows, parts, tokens, width, lanes):
    kv_width = KV_HEADS * HEAD
    part = lambda *shape: pl.BlockSpec((1, *shape), lambda i: (i,) + (0,) * len(shape))
    return call(
        functools.partial(last_body, rows, parts),
        [*[((width + kv_width, lanes), BF16)] * 2, ((rows, 2 * kv_width, tokens), BF16)],
        [
            SM, part(width, tokens), part(HALF, tokens), part(HALF, tokens), whole(1, width),
            whole(width, width), whole(kv_width, width), whole(kv_width, width),
            whole(width, width), whole(width, 1),
            *[part(kv_width, tokens)] * KV_HEADS, *[part(tokens, 2 * HEAD)] * (KV_HEADS * parts),
        ],
        [*[whole(width + kv_width, lanes)] * 2, part(2 * kv_width, tokens)],
        scratch=[pltpu.VMEM((width, width), F32), pltpu.VMEM((2 * kv_width, width), F32)],
        grid=(rows,),
        cost=estimate(2 * rows * tokens * 5.6e5, 1e7),
    )


def input_body(rows, x_ref, dmid_ref, gain_ref, wq_ref, wkv_ref, dkv_ref, *refs):
    dq_refs, ig_refs = refs[:KV_HEADS], refs[KV_HEADS:]
    step = pl.program_id(0)
    dq = jnp.concatenate([ref[0] for ref in dq_refs], axis=0)
    dnormed = mdot(wq_ref[...], dq) + mdot(wkv_ref[...], dkv_ref[0])
    x = x_ref[0].astype(F32)
    ig = (dmid_ref[0] + norm_back(x, rms_factor(x), column(gain_ref), dnormed)).astype(BF16)
    for row in range(rows):

        @pl.when(step == row)
        def _():
            ig_refs[row][...] = ig


def input_call(rows, tokens, width):
    kv_width = KV_HEADS * HEAD
    part = lambda *shape: pl.BlockSpec((1, *shape), lambda i: (i,) + (0,) * len(shape))
    return call(
        functools.partial(input_body, rows),
        [((width, tokens), BF16)] * rows,
        [
            part(width, tokens), part(width, tokens), whole(1, width), whole(width, width),
            whole(width, 2 * kv_width), part(2 * kv_width, tokens),
            *[part(kv_width, tokens)] * KV_HEADS,
        ],
        [whole(width, tokens)] * rows,
        grid=(rows,),
        cost=estimate(2 * rows * tokens * 5.6e5, 1e7),
    )


def bit_length(size):
    return [1 << i for i in range(size.bit_length() - 1)]


def swap(value, axis, bit):
    size = lax.axis_size(axis)
    return lax.ppermute(value, axis, [(i, i ^ bit) for i in range(size)])


def pick(value, index):
    return lax.dynamic_index_in_dim(value, index, 0, keepdims=False)


def after(value, *others):
    return lax.optimization_barrier((value, *others))[0]


def join(*trees):
    return lax.optimization_barrier(trees)


def place_body(count, copies, mine_ref, *refs):
    out_ref = refs[count]
    for k in range(count):
        value = refs[k][...].astype(out_ref.dtype)
        for i in range(copies):
            out_ref[i, mine_ref[0] ^ k] = value


def placed(pieces, mine, dtype=BF16, copies=1):
    count = len(pieces)
    return call(
        functools.partial(place_body, count, copies),
        [((copies, count, *pieces[0].shape), dtype)],
        [SM] + [VM] * count,
        cost=estimate(0, 2 * (1 + copies) * count * pieces[0].size),
    )(mine.reshape(1), *pieces)[0]


def unpack_body(core_ref, piece_ref, *refs):
    out_refs = refs[-3:]
    outer, inner = piece_ref.shape[:2]
    half = out_refs[0].shape[0]
    value = jnp.concatenate(
        [jnp.concatenate([piece_ref[i, j] for j in range(inner)], axis=1) for i in range(outer)],
        axis=0,
    ).astype(F32)
    for i, out_ref in enumerate(out_refs):
        out_ref[...] = value[i * half : (i + 1) * half]


def unpack(core, piece, width, hidden, sums=()):
    outer, inner, rows, lanes = piece.shape
    each = 1 if lanes % 128 == 0 else 2
    block = pl.BlockSpec((width // 2, each * lanes), lambda i, core_ref: (core_ref[0], i))
    return pl.pallas_call(
        unpack_body,
        out_shape=[jax.ShapeDtypeStruct((width, hidden), F32)] * 3,
        grid_spec=pltpu.PrefetchScalarGridSpec(
            num_scalar_prefetch=1,
            grid=(inner // each,),
            in_specs=[
                pl.BlockSpec((outer, each, rows, lanes), lambda i, core_ref: (0, i, 0, 0)),
                *[pl.BlockSpec(memory_space=pl.ANY)] * len(sums),
            ],
            out_specs=[block] * 3,
        ),
        input_output_aliases={2 + i: i for i in range(len(sums))},
        compiler_params=pltpu.CompilerParams(vmem_limit_bytes=VMEM_LIMIT),
        cost_estimate=estimate(0, 9 * width * hidden),
    )(core, piece, *sums)


def tail_body(core_ref, mine_ref, other_ref, o_ref, q_ref, k_ref, v_ref, gain_ref):
    width, kv = o_ref.shape[1], k_ref.shape[0]
    even = core_ref[0] == 0
    low = jnp.where(even, mine_ref[...], other_ref[...]).astype(F32)
    high = jnp.where(even, other_ref[...], mine_ref[...]).astype(F32)
    cut = low.shape[0] - width
    o_ref[...] = low[:width, :width]
    gain_ref[...] = low[:width, width:].T
    q_ref[:cut] = low[width:, :width]
    q_ref[cut:] = high[: width - cut, :width]
    k_ref[...] = high[width - cut : width - cut + kv, :width]
    v_ref[...] = high[width - cut + kv :, :width]


class Axis:
    def __init__(self, name, bit):
        self.name, self.bit = name, bit
        self.size = lax.axis_size(name) // bit
        self.mine = lax.axis_index(name) // bit
        self.groups = None
        if bit > 1:
            self.groups = [[c + bit * i for i in range(self.size)] for c in range(bit)]

    def trade(self, value):
        return lax.all_to_all(value, self.name, 0, 0, tiled=True, axis_index_groups=self.groups)

    def spread(self, value):
        return self.trade(jnp.broadcast_to(value, (self.size, *value.shape)))

    def send_parts(self, value):
        return [pick(value, self.mine)] + [
            swap(pick(value, self.mine ^ k), self.name, k * self.bit)
            for k in range(1, self.size)
        ]

    def send_all(self, value):
        return [value] + [swap(value, self.name, k * self.bit) for k in range(1, self.size)]


def total(pieces):
    result = pieces[0].astype(F32)
    for piece in pieces[1:]:
        result = result + piece.astype(F32)
    return result.astype(BF16)


def folded(value):
    return jnp.sum(value.astype(F32), axis=0).astype(BF16)


def split_columns(value, size):
    return jnp.swapaxes(value.reshape(value.shape[0], size, -1), 0, 1)


def shards(
    inputs, doc_lengths, gain_one, gain_two, w_query, w_key, w_value, w_out, w_gate, w_up, w_down, cotangent
):
    rows, tokens, width = inputs.shape
    hidden = w_gate.shape[1]
    seq = lax.axis_size("seq")
    batch = lax.axis_size("batch")
    parts = seq // rows
    me = lax.axis_index("seq")
    group, part = me // parts, me % parts
    wide = GROUPS * tokens
    kv_width = KV_HEADS * HEAD

    def dealt(block):
        g, place = block // parts, block % parts
        return g, place if g % 2 == 0 else parts - 1 - place

    def route(step):
        pairs = []
        for block in range(seq):
            g, p = dealt(block)
            pairs.append((block, (g ^ step) * parts + p))
        return pairs

    def bring(value):
        return [lax.ppermute(pick(value, group ^ step), "seq", route(step)) for step in range(rows)]

    def back(pieces):
        return [
            lax.ppermute(piece, "seq", [(b, a) for a, b in route(step)])
            for step, piece in enumerate(pieces)
        ]

    def place_rows(pieces, dtype):
        return jnp.swapaxes(placed(pieces, group, dtype)[0], 1, 2)

    x_parts = bring(jnp.swapaxes(inputs, 1, 2))

    groups_here = group ^ jnp.arange(rows, dtype=jnp.int32)
    blocks = groups_here * parts + jnp.where(groups_here % 2 == 0, part, parts - 1 - part)
    lengths = pick(doc_lengths, group)
    order = jnp.arange(lengths.shape[0])
    ends = jnp.sum(jnp.where(order[None, :] <= order[:, None], lengths[None, :], 0), axis=1)
    places = blocks[:, None] * tokens + jnp.arange(tokens, dtype=jnp.int32)[None, :]
    starts = jnp.sum(jnp.where(ends <= places[..., None], lengths, 0), axis=-1)
    info = jnp.concatenate(
        [
            jnp.stack([group, part]),
            jnp.stack(
                [blocks, starts[:, 0] // tokens, (starts[:, -1] + tokens - 1) // tokens], axis=1
            ).reshape(-1),
        ]
    ).astype(jnp.int32)
    inverse = 1.0 / ROPE_BASE ** (jnp.arange(HALF, dtype=F32) * (2.0 / HEAD))
    angles = (places - starts).astype(F32)[:, None, :] * inverse[None, :, None]
    cos_t, sin_t = jnp.cos(angles), jnp.sin(angles)
    gain_a = gain_one.astype(F32)[None, :]
    gain_b = gain_two.astype(F32)[None, :]
    w_pair = jnp.concatenate([w_key, w_value], axis=1)
    core = (me % 2).reshape(1)
    ready = (info, starts, cos_t, sin_t, gain_a, gain_b, w_pair, w_query.T)
    cotangent = join(cotangent, x_parts[1])[0]
    x_parts, ready = join(x_parts, ready)
    info, starts, cos_t, sin_t, gain_a, gain_b, w_pair, w_query_t = ready
    g_parts = bring(jnp.swapaxes(cotangent, 1, 2))

    x_all, normed, kv = call(
        functools.partial(pair_body, rows),
        [*[((rows, width, tokens), BF16)] * 2, ((rows, KV_HEADS, 2 * HEAD, tokens), BF16)],
        [VM] * (5 + rows),
        cost=estimate(4 * rows * tokens * width * kv_width, 3e6),
    )(gain_a, w_key.T, w_value.T, cos_t, sin_t, *x_parts)

    def ring(i, value):
        pairs = [
            (r * parts + (p + i) % parts, r * parts + p) for r in range(rows) for p in range(parts)
        ]
        return lax.ppermute(value, "seq", pairs)

    kv_all = [kv] + [ring(i, kv) for i in range(1, parts)]
    q = call(
        functools.partial(query_body, rows),
        [((rows, KV_HEADS, HEAD, wide), BF16)],
        [VM] * 4,
        cost=estimate(2 * rows * tokens * width * width, 3e6),
    )(normed, w_query_t, cos_t, sin_t)[0]
    q, kv_all = join(q, kv_all)

    attend, attend_back = attention_calls(rows, parts, tokens)
    o, lse = attend(info, starts, q, *kv_all)
    o, g_parts = join(o, g_parts)

    plane, line = Axis("seq", 2), Axis("batch", 1)
    count = rows * tokens
    *out, keep, send, grad, middle, back_acc = feed_call(rows, tokens, width, hidden, 2)(
        core, o, gain_b, w_out, w_gate, w_up, w_down.T, *x_parts, *g_parts
    )
    send, back_acc = join(send, back_acc)
    got = swap(send, "seq", 1)
    og, dmiddle, do, delta, two = turn_call(rows, tokens, width)(
        o, grad, middle, back_acc, gain_b, w_out
    )
    got, do = join(got, do)
    part = total([keep, got]).reshape(plane.size, -1, hidden)
    part, do = join(part, do)
    trade = plane.trade(part)

    def back_call(head, do):
        return attend_back(head, info, starts, cos_t, sin_t, lse, delta, do, q, *kv_all)

    def deliver(others):
        got = []
        for i, other in enumerate(others, 1):
            pairs = [
                (r * parts + p, r * parts + (p + i) % parts)
                for r in range(rows)
                for p in range(parts)
            ]
            got.append(lax.ppermute(other, "seq", pairs))
        return got

    dq0, own0, *others0 = back_call(0, do)
    dq0, do = join(dq0, do)
    got0 = deliver(others0)
    dq1, own1, *others1 = back_call(1, do)
    trade, dq1, own1, others1, do, out = join(trade, dq1, own1, others1, do, out)
    part = split_columns(folded(trade), batch)
    part, others1, do, out = join(part, others1, do, out)
    got1 = deliver(others1)
    pieces = line.trade(part)
    out_back = back(out)
    dq2, own2, *others2 = back_call(2, do)
    pieces, dq2, own2, others2, out_back = join(pieces, dq2, own2, others2, out_back)
    output = place_rows(out_back, BF16)
    part = folded(pieces)
    part, dq2, others2 = join(part, dq2, others2)
    got2 = deliver(others2)
    pieces = line.send_all(part)
    lanes = -(-width // 128) * 128
    keep, send, dkv = last_call(rows, parts, tokens, width, lanes)(
        core, normed, cos_t, sin_t, gain_a, w_query, w_key.T, w_value.T, og, two,
        dq0, dq1, dq2, own0, own1, own2, *got0, *got1, *got2,
    )
    send, dkv, keep = join(send, dkv, keep)
    got = swap(send, "seq", 1)
    ig = input_call(rows, tokens, width)(
        x_all, dmiddle, gain_a, w_query, w_pair, dkv, dq0, dq1, dq2
    )
    got, keep, ig = join(got, keep, ig)
    tail = total([keep, got]).reshape(plane.size, -1, lanes)
    tail, ig = join(tail, ig)
    trade = plane.trade(tail)
    ig_back = back(ig)
    trade, pieces, output, ig_back = join(trade, pieces, output, ig_back)
    tail = folded(trade).reshape(batch, -1, lanes)
    part = placed(pieces, line.mine, copies=plane.size)
    tail, part = join(tail, part)
    tail_pieces = line.send_parts(tail)
    feed_all = plane.trade(part)
    tail_pieces = line.send_all(total(tail_pieces))
    tail = placed(tail_pieces, line.mine)[0].reshape(-1, lanes)
    tail_pieces = plane.send_all(tail)
    input_grad = place_rows(ig_back, F32)
    tail_pieces, input_grad, feed_all = join(tail_pieces, input_grad, feed_all)
    tail_all = placed(tail_pieces, plane.mine)[0].reshape(-1, lanes)
    tail_all, feed_all = join(tail_all, feed_all)
    tail_other = swap(tail_all, "seq", 1)
    feed_other = swap(feed_all, "seq", 1)
    sums = unpack(core, feed_all, width, hidden)
    sums, tail_other, feed_other = join(sums, tail_other, feed_other)
    w_gate_sum, w_up_sum, w_down_sum = unpack(1 - core, feed_other, width, hidden, sums)
    w_out_sum, w_query_sum, w_key_sum, w_value_sum, gains = call(
        tail_body,
        [
            *[((width, width), F32)] * 2,
            *[((kv_width, width), F32)] * 2,
            ((lanes - width, width), F32),
        ],
        [SM, VM, VM],
        cost=estimate(0, 6e6),
    )(core, tail_all, tail_other)
    return (
        output,
        input_grad,
        gains[0],
        gains[1],
        w_query_sum,
        w_key_sum.T,
        w_value_sum.T,
        w_out_sum,
        w_gate_sum,
        w_up_sum,
        w_down_sum.T,
    )


def solution(mesh):
    tokens_spec = P("batch", "seq", None)
    return jax.shard_map(
        shards,
        mesh=mesh,
        in_specs=(tokens_spec, P("batch", None), *([P()] * 9), tokens_spec),
        out_specs=(tokens_spec, tokens_spec, *([P()] * 9)),
        check_vma=False,
    )
```

```python
import functools
import math

import jax
import jax.numpy as jnp
from jax import lax
from jax.experimental import pallas as pl
from jax.experimental.pallas import tpu as pltpu
from jax.sharding import PartitionSpec as P

HEADS = 9
KV_HEADS = 3
HEAD = 64
GROUPS = HEADS // KV_HEADS
HALF = HEAD // 2
EPSILON = 1e-05
ROPE_BASE = 10000.0
FAR_NEGATIVE = -1e30
SUM_ROWS = 16

F32 = jnp.float32
BF16 = jnp.bfloat16
VMEM_LIMIT = 56 * 1024 * 1024


def rms_factor(values):
    return lax.rsqrt(jnp.mean(values * values, axis=0, keepdims=True) + EPSILON)


def norm_back(source, factor, gain_value, upstream):
    scaled = upstream * gain_value
    return factor * scaled - source * factor * factor * factor * jnp.mean(
        scaled * source, axis=0, keepdims=True
    )


def mdot(left, right):
    return jnp.dot(left, right, preferred_element_type=F32)


def tdot(left, right):
    return lax.dot_general(left, right, (((0,), (0,)), ((), ())), preferred_element_type=F32)


def rdot(left, right):
    return lax.dot_general(left, right, (((1,), (1,)), ((), ())), preferred_element_type=F32)


VM = pl.BlockSpec(memory_space=pltpu.VMEM)
SM = pl.BlockSpec(memory_space=pltpu.SMEM)


def call(body, outs, in_specs, out_specs=None, scratch=(), cost=None, **more):
    return pl.pallas_call(
        body,
        out_shape=[jax.ShapeDtypeStruct(*o) for o in outs],
        in_specs=in_specs,
        out_specs=out_specs or [VM] * len(outs),
        scratch_shapes=list(scratch),
        compiler_params=pltpu.CompilerParams(vmem_limit_bytes=VMEM_LIMIT),
        cost_estimate=cost,
        **more,
    )


def whole(*shape):
    return pl.BlockSpec(shape, lambda *unused: (0,) * len(shape))


def estimate(flops, nbytes, trans=0):
    return pl.CostEstimate(
        flops=int(flops), bytes_accessed=int(nbytes), transcendentals=int(trans)
    )


def pair_body(rows, gain_ref, wk_ref, wv_ref, cos_ref, sin_ref, *refs):
    gain = column(gain_ref)
    weights = jnp.concatenate([wk_ref[...], wv_ref[...]], axis=0)
    x_refs, (x_all, normed_ref, kv_ref) = refs[:rows], refs[rows:]
    for row in range(rows):
        x_all[row] = x_refs[row][...]
        x = x_refs[row][...].astype(F32)
        normed = (x * rms_factor(x) * gain).astype(BF16)
        normed_ref[row] = normed
        turned = mdot(weights, normed)
        cos, sin = cos_ref[row], sin_ref[row]
        for head in range(KV_HEADS):
            at = head * HEAD
            a, b = turned[at : at + HALF], turned[at + HALF : at + HEAD]
            kv_ref[row, head, :HALF, :] = (a * cos - b * sin).astype(BF16)
            kv_ref[row, head, HALF:HEAD, :] = (b * cos + a * sin).astype(BF16)
            at += KV_HEADS * HEAD
            kv_ref[row, head, HEAD:, :] = turned[at : at + HEAD].astype(BF16)


def query_body(rows, normed_ref, w_ref, cos_ref, sin_ref, q_ref):
    tokens = normed_ref.shape[-1]
    for row in range(rows):
        turned = mdot(w_ref[...], normed_ref[row])
        cos, sin = cos_ref[row] * 0.125, sin_ref[row] * 0.125
        for head in range(HEADS):
            a = turned[head * HEAD : head * HEAD + HALF]
            b = turned[head * HEAD + HALF : (head + 1) * HEAD]
            kv, lane = head // GROUPS, (head % GROUPS) * tokens
            q_ref[row, kv, :HALF, lane : lane + tokens] = (a * cos - b * sin).astype(BF16)
            q_ref[row, kv, HALF:, lane : lane + tokens] = (b * cos + a * sin).astype(BF16)


def owner(block, parts):
    group, place = block // parts, block % parts
    return jnp.where(group % 2 == 0, place, parts - 1 - place)


def slot_of(block, info, parts, rows):
    relative = (owner(block, parts) - info[1] + parts) % parts
    return relative * rows + ((block // parts) ^ info[0])


def spans_of(starts_ref, row, mine):
    start = jnp.concatenate([starts_ref[pl.ds(row, 1), :]] * GROUPS, axis=1)
    tokens = starts_ref.shape[1]
    lane = lax.broadcasted_iota(jnp.int32, start.shape, 1)
    return start, mine * tokens + lane % tokens


def visible(block, start, place, shape):
    key_place = block * shape[0] + lax.broadcasted_iota(jnp.int32, shape, 0)
    return (key_place >= start) & (key_place <= place)


def attend_body(parts, rows, info_ref, start_ref, q_ref, *refs):
    kv_refs, refs = refs[:parts], refs[parts:]
    o_ref, lse_ref, k_nat, v_aug, acc = refs
    tokens = kv_refs[0].shape[-1]
    info = (info_ref[0], info_ref[1])
    ones = (lax.broadcasted_iota(jnp.int32, (SUM_ROWS, tokens), 0) == 0).astype(BF16)
    for slot in range(rows * parts):
        kv_ref = kv_refs[slot // rows].at[slot % rows]
        for head in range(KV_HEADS):
            k_nat[slot, head] = kv_ref[head, :HEAD, :].T
            v_aug[slot, head, :HEAD, :] = kv_ref[head, HEAD:, :]
            v_aug[slot, head, HEAD:, :] = ones

    def per_row(row, carry):
        mine, low, full = info_ref[2 + 3 * row], info_ref[3 + 3 * row], info_ref[4 + 3 * row]
        acc[...] = jnp.zeros_like(acc)
        start, place = spans_of(start_ref, row, mine)

        def step(block, tops, masked, count=1):
            slots = [slot_of(block + i, info, parts, rows) for i in range(count)]
            shape = (count * tokens, start.shape[-1])
            if masked:
                key_place = block * tokens + lax.broadcasted_iota(jnp.int32, shape, 0)
                allowed = (key_place >= start) & (key_place <= place)
            result = []
            for head in range(KV_HEADS):
                keys = jnp.concatenate([k_nat[slot, head] for slot in slots], axis=0)
                values = jnp.concatenate([v_aug[slot, head] for slot in slots], axis=1)
                scores = mdot(keys, q_ref[row, head])
                if masked:
                    scores = jnp.where(allowed, scores, FAR_NEGATIVE)
                top = jnp.maximum(tops[head], jnp.max(scores, axis=0, keepdims=True))
                weights = jnp.exp(scores - top).astype(BF16)
                acc[head] = acc[head] * jnp.exp(tops[head] - top) + mdot(values, weights)
                result.append(top)
            return tuple(result)

        tops = tuple(
            jnp.full((1, start.shape[-1]), FAR_NEGATIVE, F32) for unused in range(KV_HEADS)
        )
        middle = jnp.minimum(full, mine)
        tops = lax.fori_loop(low, middle, lambda b, s: step(b, s, True), tops)
        pairs = (mine - middle) // 2
        tops = lax.fori_loop(0, pairs, lambda i, s: step(middle + 2 * i, s, False, 2), tops)
        tops = lax.cond(
            (mine - middle) % 2 == 1,
            lambda s: step(mine - 1, s, True, 2),
            lambda s: step(mine, s, True),
            tops,
        )
        for head in range(KV_HEADS):
            mass = acc[head, HEAD : HEAD + 1, :]
            o_ref[row, head] = (acc[head, :HEAD, :] / mass).astype(BF16)
            lse_ref[row, head] = tops[head] + jnp.log(mass)
        return carry

    lax.fori_loop(0, rows, per_row, 0)


def attend_back_body(parts, rows, info_ref, start_ref, cos_ref, sin_ref, lse_ref, delta_ref, do_ref, q_ref, *refs):
    kv_refs, refs = refs[:parts], refs[parts:]
    dq_ref, own_ref = refs[:2]
    other_refs = refs[2 : 1 + parts]
    k_nat, v_nat, k_turned, pair, dq_acc, dkv = refs[1 + parts :]
    tokens = kv_refs[0].shape[-1]
    wide = GROUPS * tokens
    info = (info_ref[0], info_ref[1])
    for slot in range(rows * parts):
        k_turned[slot] = kv_refs[slot // rows][slot % rows, 0, :HEAD, :]
        k_nat[slot] = k_turned[slot].T
        v_nat[slot] = kv_refs[slot // rows][slot % rows, 0, HEAD:, :].T
    dkv[...] = jnp.zeros_like(dkv)
    blank = jnp.zeros((wide, HEAD), BF16)

    def per_row(row, carry):
        mine, low, full = info_ref[2 + 3 * row], info_ref[3 + 3 * row], info_ref[4 + 3 * row]
        dq_acc[...] = jnp.zeros_like(dq_acc)
        start, place = spans_of(start_ref, row, mine)
        pair[:wide, :] = jnp.concatenate([q_ref[row, 0].T, blank], axis=1)
        pair[wide:, :] = jnp.concatenate([blank, do_ref[row, 0].T], axis=1)

        def step(block, count, masked):
            slots = [slot_of(block + k, info, parts, rows) for k in range(count)]
            scores = mdot(jnp.concatenate([k_nat[slot] for slot in slots], axis=0), q_ref[row, 0])
            back = mdot(jnp.concatenate([v_nat[slot] for slot in slots], axis=0), do_ref[row, 0])
            weights = jnp.exp(scores - lse_ref[row, 0])
            if masked:
                key_place = block * tokens + lax.broadcasted_iota(jnp.int32, scores.shape, 0)
                allowed = (key_place >= start) & (key_place <= place)
                weights = jnp.where(allowed, weights, 0.0)
            slope = (weights * (back - delta_ref[row, 0])).astype(BF16)
            update = mdot(jnp.concatenate([slope, weights.astype(BF16)], axis=1), pair[...])
            for k, slot in enumerate(slots):
                dkv[slot] += update[k * tokens : (k + 1) * tokens]
            turned = jnp.concatenate([k_turned[slot] for slot in slots], axis=1)
            dq_acc[...] += mdot(turned, slope)

        def loop(first, count, times, masked):
            def once(index, carry):
                step(first + index * count, count, masked)
                return carry

            lax.fori_loop(0, times, once, 0)

        middle = jnp.minimum(full, mine)
        left = mine - middle
        loop(low, 1, middle - low, True)
        loop(middle, 2, left // 2, False)

        @pl.when(left % 2 == 1)
        def _():
            step(mine - 1, 2, True)

        @pl.when(left % 2 == 0)
        def _():
            step(mine, 1, True)

        cos, sin = cos_ref[row], sin_ref[row]
        for group in range(GROUPS):
            lanes = slice(group * tokens, (group + 1) * tokens)
            a = dq_acc[:HALF, lanes] * 0.125
            b = dq_acc[HALF:, lanes] * 0.125
            dq_ref[row, group * HEAD : group * HEAD + HALF, :] = (a * cos + b * sin).astype(BF16)
            dq_ref[row, group * HEAD + HALF : (group + 1) * HEAD, :] = (b * cos - a * sin).astype(BF16)
        return carry

    lax.fori_loop(0, rows, per_row, 0)
    own_ref[...] = dkv[:rows]
    for i, other_ref in enumerate(other_refs):
        other_ref[...] = dkv[(i + 1) * rows : (i + 2) * rows].astype(BF16)


def attention_calls(rows, parts, tokens):
    wide = GROUPS * tokens
    slots = rows * parts
    pair_work = rows * (slots + 1) / 2 * tokens * tokens * HEADS * HEAD
    attend = call(
        functools.partial(attend_body, parts, rows),
        [((rows, KV_HEADS, HEAD, wide), BF16), ((rows, KV_HEADS, 1, wide), F32)],
        [SM] + [VM] * (2 + parts),
        scratch=[
            pltpu.VMEM((slots, KV_HEADS, tokens, HEAD), BF16),
            pltpu.VMEM((slots, KV_HEADS, HEAD + SUM_ROWS, tokens), BF16),
            pltpu.VMEM((KV_HEADS, HEAD + SUM_ROWS, wide), F32),
        ],
        cost=estimate(4 * 4 * pair_work, 4e6, pair_work / HEAD),
    )

    def attend_back(head, *args):
        one_head = lambda *shape: pl.BlockSpec(
            (rows, 1, *shape), lambda i: (0, head) + (0,) * len(shape)
        )
        return call(
            functools.partial(attend_back_body, parts, rows),
            [
                ((rows, GROUPS * HEAD, tokens), BF16),
                ((rows, tokens, 2 * HEAD), F32),
                *[((rows, tokens, 2 * HEAD), BF16)] * (parts - 1),
            ],
            [
                SM, whole(rows, tokens), whole(rows, HALF, tokens),
                whole(rows, HALF, tokens), one_head(1, wide), one_head(1, wide),
                one_head(HEAD, wide), one_head(HEAD, wide), *[one_head(2 * HEAD, tokens)] * parts,
            ],
            [whole(rows, GROUPS * HEAD, tokens)] + [whole(rows, tokens, 2 * HEAD)] * parts,
            scratch=[
                pltpu.VMEM((slots, tokens, HEAD), BF16),
                pltpu.VMEM((slots, tokens, HEAD), BF16),
                pltpu.VMEM((slots, HEAD, tokens), BF16),
                pltpu.VMEM((2 * wide, 2 * HEAD), BF16),
                pltpu.VMEM((HEAD, wide), F32),
                pltpu.VMEM((slots, tokens, 2 * HEAD), F32),
            ],
            grid=(1,),
            cost=estimate(10 * 4 * pair_work / KV_HEADS, 3e6, pair_work / HEAD / KV_HEADS),
        )(*args)

    return attend, attend_back


def column(ref):
    return jnp.broadcast_to(ref[...], (8, ref.shape[1])).T[:, :1]


def keep_and_send(core, first, second):
    return jnp.where(core == 0, first, second), jnp.where(core == 0, second, first)


def feed_body(rows, core_ref, o_ref, gain_ref, wo_ref, wg_ref, wu_ref, wd_ref, *refs):
    x_refs, g_refs, refs = refs[:rows], refs[rows : 2 * rows], refs[2 * rows :]
    out_refs, refs = refs[:rows], refs[rows:]
    keep_ref, send_ref, grad, middle, back_acc, out_acc, normed, hid, dgate, dup = refs
    tokens = x_refs[0].shape[1]
    step = pl.program_id(0)
    spans = [slice(row * tokens, (row + 1) * tokens) for row in range(rows)]

    @pl.when(step == 0)
    def _():
        turned = wo_ref[...].T
        gain = column(gain_ref)
        for row, lanes in enumerate(spans):
            grad[:, lanes] = g_refs[row][...]
            mixed = jnp.concatenate(
                [
                    o_ref[row, head // GROUPS, :, (head % GROUPS) * tokens : (head % GROUPS + 1) * tokens]
                    for head in range(HEADS)
                ],
                axis=0,
            )
            total = x_refs[row][...].astype(F32) + mdot(turned, mixed)
            middle[:, lanes] = total
            out_acc[:, lanes] = total
            normed[:, lanes] = (total * rms_factor(total) * gain).astype(BF16)
        back_acc[...] = jnp.zeros_like(back_acc)

    wg_t, wu_t, wd_t = wg_ref[...].T, wu_ref[...].T, wd_ref[...].T
    for lanes in spans:
        source = normed[:, lanes]
        gate, up = mdot(wg_t, source), mdot(wu_t, source)
        dhidden = mdot(wd_t, grad[:, lanes])
        sig = jax.nn.sigmoid(gate)
        silu = gate * sig
        hid[:, lanes] = (silu * up).astype(BF16)
        dgate[:, lanes] = (dhidden * up * (sig + silu * (1.0 - sig))).astype(BF16)
        dup[:, lanes] = (dhidden * silu).astype(BF16)
    for lanes in spans:
        out_acc[:, lanes] += mdot(wd_ref[...], hid[:, lanes])
        back_acc[:, lanes] += mdot(wg_ref[...], dgate[:, lanes]) + mdot(wu_ref[...], dup[:, lanes])
    half = keep_ref.shape[0] // 3
    for i, (left, right) in enumerate(((normed, dgate), (normed, dup), (grad, hid))):
        value = rdot(left[...], right[...]).astype(BF16)
        span = slice(i * half, (i + 1) * half)
        keep_ref[span], send_ref[span] = keep_and_send(core_ref[0], value[:half], value[half:])

    @pl.when(step == pl.num_programs(0) - 1)
    def _():
        for out_ref, lanes in zip(out_refs, spans):
            out_ref[...] = out_acc[:, lanes].astype(BF16)


def feed_call(rows, tokens, width, hidden, chunks):
    count, wide, chunk = rows * tokens, GROUPS * tokens, hidden // chunks
    columns = pl.BlockSpec((width, chunk), lambda i: (0, i))
    half = pl.BlockSpec((3 * width // 2, chunk), lambda i: (0, i))
    return call(
        functools.partial(feed_body, rows),
        [
            *[((width, tokens), BF16)] * rows, *[((3 * width // 2, hidden), BF16)] * 2,
            ((width, count), BF16), *[((width, count), F32)] * 2,
        ],
        [
            SM, whole(rows, KV_HEADS, HEAD, wide), whole(1, width), whole(width, width),
            columns, columns, columns, *[whole(width, tokens)] * (2 * rows),
        ],
        [*[whole(width, tokens)] * rows, half, half, *[whole(width, count)] * 3],
        scratch=[
            pltpu.VMEM((width, count), F32), pltpu.VMEM((width, count), BF16), *[pltpu.VMEM((chunk, count), BF16)] * 3,
        ],
        grid=(chunks,),
        cost=estimate(2 * count * 9 * width * hidden, 3e7, count * hidden),
    )


def turn_body(rows, o_ref, grad, middle, back_acc, gain_ref, wo_ref, *refs):
    og_ref, dmid_ref, do_ref, delta_ref, two_ref, branches = refs
    tokens = dmid_ref.shape[-1]
    step = pl.program_id(0)
    gain = column(gain_ref)
    source = middle[...]
    dnormed = back_acc[...]
    scale = rms_factor(source)
    two = jnp.sum(dnormed * source * scale, axis=1, keepdims=True)
    dmiddle = grad[...].astype(F32) + norm_back(source, scale, gain, dnormed)
    dmid_ref[0] = dmiddle
    branch = dmiddle.astype(BF16)
    dattended = mdot(wo_ref[...], branch).astype(BF16)
    mixed = jnp.concatenate(
        [
            o_ref[0, head // GROUPS, :, (head % GROUPS) * tokens : (head % GROUPS + 1) * tokens]
            for head in range(HEADS)
        ],
        axis=0,
    )
    product = dattended.astype(F32) * mixed.astype(F32)
    for head in range(HEADS):
        kv, lane = head // GROUPS, (head % GROUPS) * tokens
        span = slice(head * HEAD, (head + 1) * HEAD)
        do_ref[0, kv, :, lane : lane + tokens] = dattended[span]
        delta_ref[0, kv, :, lane : lane + tokens] = jnp.sum(product[span], axis=0, keepdims=True)
    og = rdot(mixed, branch)

    @pl.when(step == 0)
    def _():
        two_ref[...] = two
        branches[...] = og

    @pl.when(step > 0)
    def _():
        two_ref[...] += two
        branches[...] += og

    @pl.when(step == rows - 1)
    def _():
        og_ref[...] = branches[...].astype(BF16)


def turn_call(rows, tokens, width):
    count, wide = rows * tokens, GROUPS * tokens
    block = pl.BlockSpec((width, tokens), lambda i: (0, i))
    part = lambda *shape: pl.BlockSpec((1, *shape), lambda i: (i,) + (0,) * len(shape))
    return call(
        functools.partial(turn_body, rows),
        [
            ((width, width), BF16),
            ((rows, width, tokens), F32),
            ((rows, KV_HEADS, HEAD, wide), BF16),
            ((rows, KV_HEADS, 1, wide), F32),
            ((width, 1), F32),
        ],
        [part(KV_HEADS, HEAD, wide), *[block] * 3, whole(1, width), whole(width, width)],
        [
            whole(width, width), part(width, tokens),
            part(KV_HEADS, HEAD, wide), part(KV_HEADS, 1, wide), whole(width, 1),
        ],
        scratch=[pltpu.VMEM((width, width), F32)],
        grid=(rows,),
        cost=estimate(4 * count * width * width, 1.2e7),
    )


def last_body(rows, parts, core_ref, normed_ref, cos_ref, sin_ref, gain_ref, wq_ref, wk_ref, wv_ref, og_ref, two_ref, *refs):
    dq_refs, refs = refs[:KV_HEADS], refs[KV_HEADS:]
    own_refs, refs = refs[:KV_HEADS], refs[KV_HEADS:]
    other_refs, refs = refs[: KV_HEADS * (parts - 1)], refs[KV_HEADS * (parts - 1) :]
    keep_ref, send_ref, dkv_ref, query_acc, pair_acc = refs
    step = pl.program_id(0)
    width = normed_ref.shape[1]

    @pl.when(step == 0)
    def _():
        query_acc[...] = jnp.zeros_like(query_acc)
        pair_acc[...] = jnp.zeros_like(pair_acc)

    dq = jnp.concatenate([ref[0] for ref in dq_refs], axis=0)
    cos, sin = cos_ref[0], sin_ref[0]
    keys, values = [], []
    for head in range(KV_HEADS):
        turned = own_refs[head][0]
        for i in range(parts - 1):
            turned = turned + other_refs[head * (parts - 1) + i][0].astype(F32)
        turned = turned.T
        a, b = turned[:HALF], turned[HALF:HEAD]
        keys += [a * cos + b * sin, b * cos - a * sin]
        values.append(turned[HEAD:])
    dkv = jnp.concatenate(keys + values, axis=0).astype(BF16)
    dkv_ref[0] = dkv
    normed = normed_ref[0]
    query_acc[...] += rdot(normed, dq)
    pair_acc[...] += rdot(dkv, normed)

    @pl.when(step == pl.num_programs(0) - 1)
    def _():
        one = jnp.sum(wq_ref[...].astype(F32) * query_acc[...], axis=1, keepdims=True)
        weights = jnp.concatenate([wk_ref[...], wv_ref[...]], axis=0).astype(F32)
        more = jnp.sum(weights * pair_acc[...], axis=0, keepdims=True)
        one = (one + jnp.broadcast_to(more, (8, width)).T[:, :1]) / column(gain_ref)
        query, pair = query_acc[...].astype(BF16), pair_acc[...].astype(BF16)
        half = keep_ref.shape[0]
        cut = half - width
        spare = keep_ref.shape[1] - width
        lane = lax.broadcasted_iota(jnp.int32, (width, spare), 1)
        gains = jnp.where(lane == 0, one, jnp.where(lane == 1, two_ref[...], 0.0))
        blank = jnp.zeros((half, spare), BF16)
        low = jnp.concatenate([og_ref[...], query[:cut]], axis=0)
        low = jnp.concatenate(
            [low, jnp.concatenate([gains.astype(BF16), blank[:cut]], axis=0)], axis=1
        )
        high = jnp.concatenate([query[cut:], pair], axis=0)
        high = jnp.concatenate([high, blank], axis=1)
        keep_ref[...], send_ref[...] = keep_and_send(core_ref[0], low, high)


def last_call(rows, parts, tokens, width, lanes):
    kv_width = KV_HEADS * HEAD
    part = lambda *shape: pl.BlockSpec((1, *shape), lambda i: (i,) + (0,) * len(shape))
    return call(
        functools.partial(last_body, rows, parts),
        [*[((width + kv_width, lanes), BF16)] * 2, ((rows, 2 * kv_width, tokens), BF16)],
        [
            SM, part(width, tokens), part(HALF, tokens), part(HALF, tokens), whole(1, width),
            whole(width, width), whole(kv_width, width), whole(kv_width, width),
            whole(width, width), whole(width, 1),
            *[part(kv_width, tokens)] * KV_HEADS, *[part(tokens, 2 * HEAD)] * (KV_HEADS * parts),
        ],
        [*[whole(width + kv_width, lanes)] * 2, part(2 * kv_width, tokens)],
        scratch=[pltpu.VMEM((width, width), F32), pltpu.VMEM((2 * kv_width, width), F32)],
        grid=(rows,),
        cost=estimate(2 * rows * tokens * 5.6e5, 1e7),
    )


def input_body(rows, x_ref, dmid_ref, gain_ref, wq_ref, wkv_ref, dkv_ref, *refs):
    dq_refs, ig_refs = refs[:KV_HEADS], refs[KV_HEADS:]
    step = pl.program_id(0)
    dq = jnp.concatenate([ref[0] for ref in dq_refs], axis=0)
    dnormed = mdot(wq_ref[...], dq) + mdot(wkv_ref[...], dkv_ref[0])
    x = x_ref[0].astype(F32)
    ig = (dmid_ref[0] + norm_back(x, rms_factor(x), column(gain_ref), dnormed)).astype(BF16)
    for row in range(rows):

        @pl.when(step == row)
        def _():
            ig_refs[row][...] = ig


def input_call(rows, tokens, width):
    kv_width = KV_HEADS * HEAD
    part = lambda *shape: pl.BlockSpec((1, *shape), lambda i: (i,) + (0,) * len(shape))
    return call(
        functools.partial(input_body, rows),
        [((width, tokens), BF16)] * rows,
        [
            part(width, tokens), part(width, tokens), whole(1, width), whole(width, width),
            whole(width, 2 * kv_width), part(2 * kv_width, tokens),
            *[part(kv_width, tokens)] * KV_HEADS,
        ],
        [whole(width, tokens)] * rows,
        grid=(rows,),
        cost=estimate(2 * rows * tokens * 5.6e5, 1e7),
    )


def bit_length(size):
    return [1 << i for i in range(size.bit_length() - 1)]


def swap(value, axis, bit):
    size = lax.axis_size(axis)
    return lax.ppermute(value, axis, [(i, i ^ bit) for i in range(size)])


def pick(value, index):
    return lax.dynamic_index_in_dim(value, index, 0, keepdims=False)


def after(value, *others):
    return lax.optimization_barrier((value, *others))[0]


def join(*trees):
    return lax.optimization_barrier(trees)


def place_body(count, copies, mine_ref, *refs):
    out_ref = refs[count]
    for k in range(count):
        value = refs[k][...].astype(out_ref.dtype)
        for i in range(copies):
            out_ref[i, mine_ref[0] ^ k] = value


def placed(pieces, mine, dtype=BF16, copies=1):
    count = len(pieces)
    return call(
        functools.partial(place_body, count, copies),
        [((copies, count, *pieces[0].shape), dtype)],
        [SM] + [VM] * count,
        cost=estimate(0, 2 * (1 + copies) * count * pieces[0].size),
    )(mine.reshape(1), *pieces)[0]


def unpack_body(core_ref, piece_ref, *refs):
    out_refs = refs[-3:]
    outer, inner = piece_ref.shape[:2]
    half = out_refs[0].shape[0]
    value = jnp.concatenate(
        [jnp.concatenate([piece_ref[i, j] for j in range(inner)], axis=1) for i in range(outer)],
        axis=0,
    ).astype(F32)
    for i, out_ref in enumerate(out_refs):
        out_ref[...] = value[i * half : (i + 1) * half]


def unpack(core, piece, width, hidden, sums=()):
    outer, inner, rows, lanes = piece.shape
    each = 1 if lanes % 128 == 0 else 2
    block = pl.BlockSpec((width // 2, each * lanes), lambda i, core_ref: (core_ref[0], i))
    return pl.pallas_call(
        unpack_body,
        out_shape=[jax.ShapeDtypeStruct((width, hidden), F32)] * 3,
        grid_spec=pltpu.PrefetchScalarGridSpec(
            num_scalar_prefetch=1,
            grid=(inner // each,),
            in_specs=[
                pl.BlockSpec((outer, each, rows, lanes), lambda i, core_ref: (0, i, 0, 0)),
                *[pl.BlockSpec(memory_space=pl.ANY)] * len(sums),
            ],
            out_specs=[block] * 3,
        ),
        input_output_aliases={2 + i: i for i in range(len(sums))},
        compiler_params=pltpu.CompilerParams(vmem_limit_bytes=VMEM_LIMIT),
        cost_estimate=estimate(0, 9 * width * hidden),
    )(core, piece, *sums)


def tail_body(core_ref, mine_ref, other_ref, o_ref, q_ref, k_ref, v_ref, gain_ref):
    width, kv = o_ref.shape[1], k_ref.shape[0]
    even = core_ref[0] == 0
    low = jnp.where(even, mine_ref[...], other_ref[...]).astype(F32)
    high = jnp.where(even, other_ref[...], mine_ref[...]).astype(F32)
    cut = low.shape[0] - width
    o_ref[...] = low[:width, :width]
    gain_ref[...] = low[:width, width:].T
    q_ref[:cut] = low[width:, :width]
    q_ref[cut:] = high[: width - cut, :width]
    k_ref[...] = high[width - cut : width - cut + kv, :width]
    v_ref[...] = high[width - cut + kv :, :width]


class Axis:
    def __init__(self, name, bit):
        self.name, self.bit = name, bit
        self.size = lax.axis_size(name) // bit
        self.mine = lax.axis_index(name) // bit
        self.groups = None
        if bit > 1:
            self.groups = [[c + bit * i for i in range(self.size)] for c in range(bit)]

    def trade(self, value):
        return lax.all_to_all(value, self.name, 0, 0, tiled=True, axis_index_groups=self.groups)

    def spread(self, value):
        return self.trade(jnp.broadcast_to(value, (self.size, *value.shape)))

    def send_parts(self, value):
        return [pick(value, self.mine)] + [
            swap(pick(value, self.mine ^ k), self.name, k * self.bit)
            for k in range(1, self.size)
        ]

    def send_all(self, value):
        return [value] + [swap(value, self.name, k * self.bit) for k in range(1, self.size)]


def total(pieces):
    result = pieces[0].astype(F32)
    for piece in pieces[1:]:
        result = result + piece.astype(F32)
    return result.astype(BF16)


def folded(value):
    return jnp.sum(value.astype(F32), axis=0).astype(BF16)


def split_columns(value, size):
    return jnp.swapaxes(value.reshape(value.shape[0], size, -1), 0, 1)


def shards(
    inputs, doc_lengths, gain_one, gain_two, w_query, w_key, w_value, w_out, w_gate, w_up, w_down, cotangent
):
    rows, tokens, width = inputs.shape
    hidden = w_gate.shape[1]
    seq = lax.axis_size("seq")
    batch = lax.axis_size("batch")
    parts = seq // rows
    me = lax.axis_index("seq")
    group, part = me // parts, me % parts
    wide = GROUPS * tokens
    kv_width = KV_HEADS * HEAD

    def dealt(block):
        g, place = block // parts, block % parts
        return g, place if g % 2 == 0 else parts - 1 - place

    def route(step):
        pairs = []
        for block in range(seq):
            g, p = dealt(block)
            pairs.append((block, (g ^ step) * parts + p))
        return pairs

    def bring(value):
        return [lax.ppermute(pick(value, group ^ step), "seq", route(step)) for step in range(rows)]

    def back(pieces):
        return [
            lax.ppermute(piece, "seq", [(b, a) for a, b in route(step)])
            for step, piece in enumerate(pieces)
        ]

    def place_rows(pieces, dtype):
        return jnp.swapaxes(placed(pieces, group, dtype)[0], 1, 2)

    x_parts = bring(jnp.swapaxes(inputs, 1, 2))

    groups_here = group ^ jnp.arange(rows, dtype=jnp.int32)
    blocks = groups_here * parts + jnp.where(groups_here % 2 == 0, part, parts - 1 - part)
    lengths = pick(doc_lengths, group)
    order = jnp.arange(lengths.shape[0])
    ends = jnp.sum(jnp.where(order[None, :] <= order[:, None], lengths[None, :], 0), axis=1)
    places = blocks[:, None] * tokens + jnp.arange(tokens, dtype=jnp.int32)[None, :]
    starts = jnp.sum(jnp.where(ends <= places[..., None], lengths, 0), axis=-1)
    info = jnp.concatenate(
        [
            jnp.stack([group, part]),
            jnp.stack(
                [blocks, starts[:, 0] // tokens, (starts[:, -1] + tokens - 1) // tokens], axis=1
            ).reshape(-1),
        ]
    ).astype(jnp.int32)
    inverse = 1.0 / ROPE_BASE ** (jnp.arange(HALF, dtype=F32) * (2.0 / HEAD))
    angles = (places - starts).astype(F32)[:, None, :] * inverse[None, :, None]
    cos_t, sin_t = jnp.cos(angles), jnp.sin(angles)
    gain_a = gain_one.astype(F32)[None, :]
    gain_b = gain_two.astype(F32)[None, :]
    w_pair = jnp.concatenate([w_key, w_value], axis=1)
    core = (me % 2).reshape(1)
    ready = (info, starts, cos_t, sin_t, gain_a, gain_b, w_pair, w_query.T)
    cotangent = join(cotangent, x_parts[1])[0]
    x_parts, ready = join(x_parts, ready)
    info, starts, cos_t, sin_t, gain_a, gain_b, w_pair, w_query_t = ready
    g_parts = bring(jnp.swapaxes(cotangent, 1, 2))

    x_all, normed, kv = call(
        functools.partial(pair_body, rows),
        [*[((rows, width, tokens), BF16)] * 2, ((rows, KV_HEADS, 2 * HEAD, tokens), BF16)],
        [VM] * (5 + rows),
        cost=estimate(4 * rows * tokens * width * kv_width, 3e6),
    )(gain_a, w_key.T, w_value.T, cos_t, sin_t, *x_parts)

    def ring(i, value):
        pairs = [
            (r * parts + (p + i) % parts, r * parts + p) for r in range(rows) for p in range(parts)
        ]
        return lax.ppermute(value, "seq", pairs)

    kv_all = [kv] + [ring(i, kv) for i in range(1, parts)]
    q = call(
        functools.partial(query_body, rows),
        [((rows, KV_HEADS, HEAD, wide), BF16)],
        [VM] * 4,
        cost=estimate(2 * rows * tokens * width * width, 3e6),
    )(normed, w_query_t, cos_t, sin_t)[0]
    q, kv_all = join(q, kv_all)

    attend, attend_back = attention_calls(rows, parts, tokens)
    o, lse = attend(info, starts, q, *kv_all)
    o, g_parts = join(o, g_parts)

    plane, line = Axis("seq", 2), Axis("batch", 1)
    count = rows * tokens
    *out, keep, send, grad, middle, back_acc = feed_call(rows, tokens, width, hidden, 3)(
        core, o, gain_b, w_out, w_gate, w_up, w_down.T, *x_parts, *g_parts
    )
    send, back_acc = join(send, back_acc)
    got = swap(send, "seq", 1)
    og, dmiddle, do, delta, two = turn_call(rows, tokens, width)(
        o, grad, middle, back_acc, gain_b, w_out
    )
    got, do = join(got, do)
    part = total([keep, got]).reshape(plane.size, -1, hidden)
    part, do = join(part, do)
    trade = plane.trade(part)

    def back_call(head, do):
        return attend_back(head, info, starts, cos_t, sin_t, lse, delta, do, q, *kv_all)

    def deliver(others):
        got = []
        for i, other in enumerate(others, 1):
            pairs = [
                (r * parts + p, r * parts + (p + i) % parts)
                for r in range(rows)
                for p in range(parts)
            ]
            got.append(lax.ppermute(other, "seq", pairs))
        return got

    dq0, own0, *others0 = back_call(0, do)
    dq0, do = join(dq0, do)
    got0 = deliver(others0)
    dq1, own1, *others1 = back_call(1, do)
    trade, dq1, own1, others1, do, out = join(trade, dq1, own1, others1, do, out)
    part = split_columns(folded(trade), batch)
    part, others1, do, out = join(part, others1, do, out)
    got1 = deliver(others1)
    pieces = line.trade(part)
    out_back = back(out)
    dq2, own2, *others2 = back_call(2, do)
    pieces, dq2, own2, others2, out_back = join(pieces, dq2, own2, others2, out_back)
    output = place_rows(out_back, BF16)
    part = folded(pieces)
    part, dq2, others2 = join(part, dq2, others2)
    got2 = deliver(others2)
    pieces = line.send_all(part)
    lanes = -(-width // 128) * 128
    keep, send, dkv = last_call(rows, parts, tokens, width, lanes)(
        core, normed, cos_t, sin_t, gain_a, w_query, w_key.T, w_value.T, og, two,
        dq0, dq1, dq2, own0, own1, own2, *got0, *got1, *got2,
    )
    send, dkv, keep = join(send, dkv, keep)
    got = swap(send, "seq", 1)
    ig = input_call(rows, tokens, width)(
        x_all, dmiddle, gain_a, w_query, w_pair, dkv, dq0, dq1, dq2
    )
    got, keep, ig = join(got, keep, ig)
    tail = total([keep, got]).reshape(plane.size, -1, lanes)
    tail, ig = join(tail, ig)
    trade = plane.trade(tail)
    ig_back = back(ig)
    trade, pieces, output, ig_back = join(trade, pieces, output, ig_back)
    tail = folded(trade).reshape(batch, -1, lanes)
    part = placed(pieces, line.mine, copies=plane.size)
    tail, part = join(tail, part)
    tail_pieces = line.send_parts(tail)
    feed_all = plane.trade(part)
    tail_pieces = line.send_all(total(tail_pieces))
    tail = placed(tail_pieces, line.mine)[0].reshape(-1, lanes)
    tail_pieces = plane.send_all(tail)
    input_grad = place_rows(ig_back, F32)
    tail_pieces, input_grad, feed_all = join(tail_pieces, input_grad, feed_all)
    tail_all = placed(tail_pieces, plane.mine)[0].reshape(-1, lanes)
    tail_all, feed_all = join(tail_all, feed_all)
    tail_other = swap(tail_all, "seq", 1)
    feed_other = swap(feed_all, "seq", 1)
    sums = unpack(core, feed_all, width, hidden)
    sums, tail_other, feed_other = join(sums, tail_other, feed_other)
    w_gate_sum, w_up_sum, w_down_sum = unpack(1 - core, feed_other, width, hidden, sums)
    w_out_sum, w_query_sum, w_key_sum, w_value_sum, gains = call(
        tail_body,
        [
            *[((width, width), F32)] * 2,
            *[((kv_width, width), F32)] * 2,
            ((lanes - width, width), F32),
        ],
        [SM, VM, VM],
        cost=estimate(0, 6e6),
    )(core, tail_all, tail_other)
    return (
        output,
        input_grad,
        gains[0],
        gains[1],
        w_query_sum,
        w_key_sum.T,
        w_value_sum.T,
        w_out_sum,
        w_gate_sum,
        w_up_sum,
        w_down_sum.T,
    )


def solution(mesh):
    tokens_spec = P("batch", "seq", None)
    return jax.shard_map(
        shards,
        mesh=mesh,
        in_specs=(tokens_spec, P("batch", None), *([P()] * 9), tokens_spec),
        out_specs=(tokens_spec, tokens_spec, *([P()] * 9)),
        check_vma=False,
    )
```
